512 devices in a mesh: step: 2 (over core), lat: 8 (over y, x_hi), lon: 32 (over x_lo, z).
Axes of the slice: x: 4 (x_hi: 2, x_lo: 2; x = x_hi * 2 + x_lo), y: 4, z: 16, core: 2. Of those that a mesh axis runs over, the one named last changes fastest.
Arguments:
- states: bfloat16 [2, 2, 48, 384, 512], P('step', None, 'lat', 'lon'), may hold values from -6 to 6
- final_cot: bfloat16 [2, 48, 384, 512], P(None, 'lat', 'lon'), may hold values from -6 to 6
- step_cot: bfloat16 [2, 48, 384, 512], P(None, 'lat', 'lon'), may hold values from -6 to 6
- w_qkv: bfloat16 [512, 1536], replicated, may hold values from -0.25 to 0.25
- w_out: bfloat16 [512, 512], replicated, may hold values from -0.25 to 0.25
- land_vec: float32 [512], replicated, may hold values from -6 to 6
- land_sea: int32 [48, 384], replicated, may hold values 0 or 1
- ground_level: int32 [48, 384], replicated, may hold values from 0 to 1
- shift_offsets: int32 [2, 2], replicated, may hold values from 1 to 11, as said below
Outputs:
- gradients: bfloat16 [2, 2, 48, 384, 512], P('step', None, 'lat', 'lon')
The draws below stay inside these ranges and needn't reach their ends.
Inputs may be any that keep to these rules, and one draw needn't show every extreme that they name: `shift_offsets`: row k holds the shifts of the layer applied to state k: latitude from 1 to 5, longitude from 1 to 11; in each column one of the two rows holds that column's largest value.
All inputs are finite; a program needn't handle non-finite values.
Results may differ from the reference program's by a relative error of at most 0.011.
Values may be sent and summed in bfloat16 or wider, within the bound.
A program may use at most 64 MiB of HBM per device.

```python
import jax
import jax.numpy as jnp
from jax import lax

D = 512
HEADS = 8
LEV = 2
WLAT = 6
WLON = 12
LAT = 48
LON = 384


def draw_shift_offsets(key, part):
    key = jax.random.fold_in(key, 7)
    keys_all = jax.random.split(key, 4)
    lat_other = jax.random.randint(keys_all[0], (), 1, WLAT)
    lon_other = jax.random.randint(keys_all[1], (), 1, WLON)
    lat_first = jax.random.randint(keys_all[2], (), 0, 2)
    lon_first = jax.random.randint(keys_all[3], (), 0, 2)
    steps_ids = jnp.arange(2, dtype=jnp.int32)
    lat_shift = jnp.where(steps_ids == lat_first, WLAT - 1, lat_other)
    lon_shift = jnp.where(steps_ids == lon_first, WLON - 1, lon_other)
    return jnp.stack([lat_shift, lon_shift], axis=1).astype(jnp.int32)


def with_ends(drawn, rng, low, high):
    longest = drawn.shape.index(max(drawn.shape))
    spots = []
    for shift in (0, 1):
        where = [jax.random.randint(jax.random.fold_in(rng, axis), (), 0, length) for axis, length in enumerate(drawn.shape)]
        where[longest] = (where[longest] + shift) % drawn.shape[longest]
        spots.append(tuple(where))
    return drawn.at[spots[0]].set(low).at[spots[1]].set(high)


def block_scale(own_key, shape, shards, smallest, high):
    loudness = 1.0
    for dim, blocks in shards:
        draws = jax.random.uniform(jax.random.fold_in(jax.random.fold_in(own_key, 6), dim), (blocks,), jnp.float32, smallest / len(shards), high / len(shards))
        loudness = loudness * jnp.repeat(jnp.exp(draws), shape[dim] // blocks).reshape((-1,) + (1,) * (len(shape) - 1 - dim))
    return loudness


def bell_draw(own_key, extent, scale, bound, pieces=(), held_as=jnp.bfloat16):
    array = jax.random.normal(own_key, extent, jnp.float32) * scale
    if len(pieces) > 0:
        array = block_scale(own_key, extent, pieces, -0.22, 0.18) * array
    return jnp.clip(array, min=-bound, max=bound).astype(held_as)


def setup_inputs(seed: int = 0) -> dict:
    key_of = jax.random.split(jax.random.key(seed), 10)
    states = bell_draw(key_of[0], (2, LEV, LAT, LON, D), 1.0, 6.0, ((0, 2), (2, 8), (3, 32)))
    final_cot = bell_draw(key_of[1], (LEV, LAT, LON, D), 1.0, 6.0, ((1, 8), (2, 32)))
    step_cot = bell_draw(key_of[2], (LEV, LAT, LON, D), 1.0, 6.0, ((1, 8), (2, 32)))
    w_qkv = bell_draw(key_of[3], (D, 3 * D), D ** -0.5, 0.25)
    w_out = bell_draw(key_of[4], (D, D), D ** -0.5, 0.25)
    land_vec = bell_draw(key_of[5], (D,), 1.0, 6.0, (), jnp.float32)
    land_sea = with_ends((jax.random.randint(key_of[6], (LAT, LON), 0, 3) < 1).astype(jnp.int32), jax.random.fold_in(key_of[6], 1), 0, 1)
    ground_level = with_ends(jax.random.randint(key_of[7], (LAT, LON), 0, LEV), jax.random.fold_in(key_of[7], 1), 0, LEV - 1).astype(jnp.int32)
    shift_offsets = draw_shift_offsets(jax.random.fold_in(key_of[9], 71), 0)
    return dict(states=states, final_cot=final_cot, step_cot=step_cot, w_qkv=w_qkv, w_out=w_out, land_vec=land_vec, land_sea=land_sea, ground_level=ground_level, shift_offsets=shift_offsets)


def to_windows(tensor):
    levels, height, across = (tensor.shape[0], tensor.shape[1], tensor.shape[2])
    trailing = tuple(tensor.shape[3:])
    shaped = tensor.reshape((levels, height // WLAT, WLAT, across // WLON, WLON) + trailing)
    axes_order = (1, 3, 0, 2, 4) + tuple(range(5, 5 + len(trailing)))
    return jnp.transpose(shaped, axes_order).reshape((height // WLAT * (across // WLON), levels * WLAT * WLON) + trailing)

def from_windows(tensor, levels, height, across):
    trailing = tuple(tensor.shape[2:])
    shaped = tensor.reshape((height // WLAT, across // WLON, levels, WLAT, WLON) + trailing)
    axes_order = (2, 0, 3, 1, 4) + tuple(range(5, 5 + len(trailing)))
    return jnp.transpose(shaped, axes_order).reshape((levels, height, across) + trailing)

def window_branch(state_field, land_block, ground_block, seam_rows, w_qkv, w_out, land_vec):
    levels, height, across, features = state_field.shape
    head_size = features // HEADS
    lifted = state_field + land_block[None, :, :, None] * land_vec[None, None, None, :]
    average = lax.optimization_barrier(jnp.mean(lifted, axis=-1, keepdims=True))
    centred = lifted - average
    spread = lax.optimization_barrier(jnp.mean(centred * centred, axis=-1, keepdims=True))
    normed = (centred * lax.rsqrt(spread + 1e-05)).astype(jnp.bfloat16)
    windows = to_windows(normed)
    level_ids = jnp.arange(levels, dtype=jnp.int32)[:, None, None]
    key_valid = to_windows(jnp.broadcast_to((level_ids >= ground_block[None]).astype(jnp.float32), (levels, height, across)))
    seam_all = to_windows(jnp.broadcast_to(seam_rows[None, :, None], (levels, height, across)))
    allowed = key_valid[:, None, :] * (seam_all[:, :, None] == seam_all[:, None, :]).astype(jnp.float32)
    projected = jnp.einsum('wnd,de->wne', windows.astype(jnp.float32), w_qkv.astype(jnp.float32)).astype(jnp.bfloat16)
    projected = projected.reshape(windows.shape[0], windows.shape[1], 3, HEADS, head_size)
    query_heads = projected[:, :, 0].astype(jnp.float32)
    key_heads = projected[:, :, 1].astype(jnp.float32)
    value_heads = projected[:, :, 2].astype(jnp.float32)
    scores = jnp.einsum('wnhe,wmhe->whnm', query_heads, key_heads) * head_size ** (-0.5)
    weights = jnp.exp(scores) * allowed[:, None]
    attention = (weights / lax.optimization_barrier(jnp.sum(weights, axis=-1, keepdims=True))).astype(jnp.bfloat16)
    mixed = jnp.einsum('whnm,wmhe->wnhe', attention.astype(jnp.float32), value_heads).astype(jnp.bfloat16)
    mixed = mixed.reshape(windows.shape[0], windows.shape[1], HEADS * head_size)
    branch = jnp.einsum('wnf,fd->wnd', mixed.astype(jnp.float32), w_out.astype(jnp.float32))
    return from_windows(branch, levels, height, across)

def layer_adjoint(state, cotangent, shifts, land_sea, ground_level, w_qkv, w_out, land_vec):
    shift_lat = shifts[0]
    shift_lon = shifts[1]
    lat_total = land_sea.shape[0]
    land_block = jnp.roll(land_sea.astype(jnp.float32), (-shift_lat, -shift_lon), axis=(0, 1))
    ground_block = jnp.roll(ground_level, (-shift_lat, -shift_lon), axis=(0, 1))
    seam_rows = (jnp.arange(lat_total, dtype=jnp.int32) >= lat_total - shift_lat).astype(jnp.float32)

    def branch_of(state_field):
        rolled = jnp.roll(state_field, (-shift_lat, -shift_lon), axis=(1, 2))
        branch = window_branch(rolled, land_block, ground_block, seam_rows, w_qkv, w_out, land_vec)
        return jnp.roll(branch, (shift_lat, shift_lon), axis=(1, 2))
    _, pullback = jax.vjp(branch_of, state.astype(jnp.float32))
    return cotangent + pullback(cotangent)[0]

def reference(states, final_cot, step_cot, w_qkv, w_out, land_vec, land_sea, ground_level, shift_offsets):
    final_grad = final_cot.astype(jnp.float32)
    later_grad = (step_cot.astype(jnp.float32) + layer_adjoint(states[1], final_grad, shift_offsets[1], land_sea, ground_level, w_qkv, w_out, land_vec)).astype(jnp.bfloat16)
    earliest = layer_adjoint(states[0], later_grad.astype(jnp.float32), shift_offsets[0], land_sea, ground_level, w_qkv, w_out, land_vec).astype(jnp.bfloat16)
    return jnp.stack([earliest, later_grad])
```

```python
import functools

import jax
import jax.numpy as jnp
import numpy as np
from jax import lax
from jax.experimental import pallas as pl
from jax.experimental.pallas import tpu as pltpu
from jax.sharding import PartitionSpec as P

HEADS = 8
LEV = 2
WLAT = 6
WLON = 12
TOK = WLAT * WLON * LEV
MESH = pl.DeviceIdType.MESH
F32 = jnp.float32
BF16 = jnp.bfloat16
NT = (((1,), (1,)), ((), ()))
TN = (((0,), (0,)), ((), ()))


def up_to(value, unit):
    return -(-value // unit) * unit


class Exchange:
    def __init__(self, first_rows, last_rows, first_cols, last_cols):
        rows = {-1: range(first_rows), 0: range(WLAT), 1: range(WLAT - last_rows, WLAT)}
        cols = {-1: range(first_cols), 0: range(WLON), 1: range(WLON - last_cols, WLON)}
        self.pieces = []
        pack, codes = [], list(range(4 * TOK, 5 * TOK))
        offset = 0
        for dy, dx in ((1, 0), (-1, 0), (0, 1), (0, -1), (1, 1), (1, -1), (-1, 1), (-1, -1)):
            tokens = [(r * WLON + c) * LEV + l for r in rows[dy] for c in cols[dx] for l in range(LEV)]
            if not tokens:
                continue
            size = up_to(len(tokens), 16)
            zone = (1 - dy) * 3 + 1 - dx
            filler = [-1] * (size - len(tokens))
            codes += [zone * TOK + token for token in tokens] + filler
            pack += tokens + filler
            self.pieces.append((dy, dx, offset, size))
            offset += size
        self.sent = offset
        self.rows = TOK + offset
        self.padded = up_to(self.rows, 128)
        self.codes = np.array(codes + [-1] * (self.padded - self.rows), np.int32)
        self.pack = (np.array(pack)[:, None] == np.arange(TOK)[None, :]).astype(np.float32)


def frame_places():
    index = lax.broadcasted_iota(jnp.int32, (TOK, 1), 0)
    place = index >> 1
    row = (place * 43691) >> 19
    return row, place - row * WLON, index & 1


def read_codes(down, right):
    row, col, level = frame_places()
    row_at = row + down
    col_at = col + right
    zone_row = jnp.where(row_at >= WLAT, 1, 0) - jnp.where(row_at < 0, 1, 0)
    zone_col = jnp.where(col_at >= WLON, 1, 0) - jnp.where(col_at < 0, 1, 0)
    place = (row_at - zone_row * WLAT) * WLON + col_at - zone_col * WLON
    return ((zone_row + 1) * 3 + zone_col + 1) * TOK + place * LEV + level


def one_hot(left, right):
    return jnp.where(left == right, 1.0, 0.0).astype(BF16)


def dot(a, b, dims=(((1,), (0,)), ((), ()))):
    return lax.dot_general(a, b, dims, preferred_element_type=F32)


def kernel(
    sizes, halo, mid, out,
    states, final_cot, step_cot, w_qkv, w_out, land_vec, land_sea, ground, shifts,
    pack_halo, pack_mid, pack_out, codes,
    result,
    raw, w_qkv_v, w_out_v, land_vec_v, tables_v, shifts_v, pack_halo_v, pack_mid_v, pack_out_v, codes_v,
    ext_halo, ext_mid, ext_out, send_halo, send_mid, send_out,
    normed_f, proj, att, cot_w, d_proj, d_mixed,
    local_sem, send_sem, recv_sem, go_sem,
):
    n_lat, n_lon = sizes
    features = raw.shape[-1]
    step, lat, lon = lax.axis_index("step"), lax.axis_index("lat"), lax.axis_index("lon")
    late = step == 1

    def around(dy, dx, other=False):
        return (
            1 - step if other else step,
            lax.rem(lat + (dy + n_lat), n_lat),
            lax.rem(lon + (dx + n_lon), n_lon),
        )

    barrier = pltpu.get_barrier_semaphore()
    for dy in (-1, 0, 1):
        for dx in (-1, 0, 1):
            if (dy, dx) != (0, 0):
                pl.semaphore_signal(barrier, inc=1, device_id=around(dy, dx), device_id_type=MESH)
            pl.semaphore_signal(barrier, inc=1, device_id=around(dy, dx, True), device_id_type=MESH)

    local = [
        pltpu.make_async_copy(src, dst, local_sem.at[i])
        for i, (src, dst) in enumerate((
            (states, raw.at[0]),
            (pack_halo, pack_halo_v),
            (final_cot, raw.at[1]),
            (step_cot, raw.at[2]),
            (shifts, shifts_v),
            (codes, codes_v),
            (land_sea, tables_v.at[0]),
            (ground, tables_v.at[1]),
            (land_vec, land_vec_v),
            (w_qkv, w_qkv_v),
            (w_out, w_out_v),
            (pack_out, pack_out_v),
            (pack_mid, pack_mid_v),
        ))
    ]
    (c_state, c_pack, c_final, c_step, c_shift, c_codes, c_land, c_ground, c_vec, c_qkv, c_out, c_pack_out, c_pack_mid) = local
    for copy in local:
        copy.start()

    def sends(which, exchange, buffer, target, other=False):
        made = []
        base = (0, 8, 16, 24, 32)[which]
        for k, (dy, dx, offset, size) in enumerate(exchange.pieces):
            made.append(pltpu.make_async_remote_copy(
                src_ref=buffer.at[pl.ds(offset, size)],
                dst_ref=target.at[pl.ds(TOK + offset, size)],
                send_sem=send_sem.at[base + k],
                recv_sem=recv_sem.at[base + k],
                device_id=around(dy, dx, other),
                device_id_type=MESH,
            ))
        return made

    halo_sends = [sends(i, halo, send_halo.at[i], ext_halo.at[i]) for i in range(3)]
    mid_sends = sends(3, mid, send_mid, ext_mid, True)
    mid_sends.append(pltpu.make_async_remote_copy(
        src_ref=ext_out.at[pl.ds(0, TOK)],
        dst_ref=ext_mid.at[pl.ds(0, TOK)],
        send_sem=send_sem.at[40],
        recv_sem=recv_sem.at[40],
        device_id=around(0, 0, True),
        device_id_type=MESH,
    ))
    out_sends = sends(4, out, send_out, ext_out)

    def pack_field(i):
        field = raw[i].reshape(TOK, features)
        ext_halo[i, pl.ds(0, TOK)] = field
        send_halo[i] = dot(pack_halo_v[...].astype(BF16), field).astype(BF16)

    for i in range(3):
        ext_halo[i, pl.ds(halo.rows, halo.padded - halo.rows)] = jnp.zeros((halo.padded - halo.rows, raw.shape[-1]), BF16)
    ext_mid[pl.ds(mid.rows, mid.padded - mid.rows)] = jnp.zeros((mid.padded - mid.rows, raw.shape[-1]), BF16)
    ext_out[pl.ds(out.rows, out.padded - out.rows)] = jnp.zeros((out.padded - out.rows, raw.shape[-1]), BF16)

    c_state.wait()
    c_pack.wait()
    pack_field(0)
    pl.semaphore_wait(barrier, 17)

    c_final.wait()
    c_step.wait()

    @pl.when(late)
    def _():
        for copy in halo_sends[0]:
            copy.start()
        pack_field(1)
        for copy in halo_sends[1]:
            copy.start()
        pack_field(2)

    c_shift.wait()

    def start_of(row):
        a, b = shifts_v[row, 0], shifts_v[row, 1]
        return jnp.where(a >= 3, a - WLAT, a), jnp.where(b >= 6, b - WLON, b)

    s_late, t_late = start_of(1)
    s_early, t_early = start_of(0)
    s = jnp.where(late, s_late, s_early)
    t = jnp.where(late, t_late, t_early)
    c_codes.wait()
    pick_halo = one_hot(read_codes(s, t), codes_v[0:1, : halo.padded])

    row, col, level = frame_places()
    lat_total, lon_total = tables_v.shape[1], tables_v.shape[2]
    at_row = lat * WLAT + s + row
    at_row = jnp.where(at_row < 0, at_row + lat_total, jnp.where(at_row >= lat_total, at_row - lat_total, at_row))
    at_col = lon * WLON + t + col
    at_col = jnp.where(at_col < 0, at_col + lon_total, jnp.where(at_col >= lon_total, at_col - lon_total, at_col))
    c_land.wait()
    c_ground.wait()
    row_pick = one_hot(at_row, lax.broadcasted_iota(jnp.int32, (TOK, lat_total), 1))
    col_pick = at_col == lax.broadcasted_iota(jnp.int32, (TOK, lon_total), 1)

    def looked_up(i):
        lines = dot(row_pick, tables_v[i].astype(F32).astype(BF16))
        return jnp.sum(jnp.where(col_pick, lines, 0.0), axis=1, keepdims=True)

    land = looked_up(0)
    key_valid = jnp.where(level.astype(F32) >= looked_up(1), 1.0, 0.0)
    shift_lat = jnp.where(s < 0, s + WLAT, s)
    window = jnp.where(s < 0, lax.rem(lat + (n_lat - 1), n_lat), lat)
    first_seam = jnp.where(window == n_lat - 1, WLAT - shift_lat, WLAT)
    lane = lax.broadcasted_iota(jnp.int32, (1, 2 * TOK), 1)
    lane = jnp.where(lane >= TOK, lane - TOK, lane)
    lane_row = ((lane >> 1) * 43691) >> 19
    seam_key = jnp.where(row >= first_seam, 1, 0)
    seam_query = jnp.where(lane_row >= first_seam, 1, 0)
    allowed = jnp.where(seam_key == seam_query, key_valid, 0.0)
    c_vec.wait()

    @pl.when(late)
    def _():
        for copy in halo_sends[0]:
            copy.wait_recv()
        pl.semaphore_signal(go_sem, inc=1, device_id=around(0, 0, True), device_id_type=MESH)

    @pl.when(jnp.logical_not(late))
    def _():
        pl.semaphore_wait(go_sem, 1)
        for copy in halo_sends[0]:
            copy.start()
        for copy in halo_sends[0]:
            copy.wait_recv()

    lifted = dot(pick_halo, ext_halo[0]) + land * land_vec_v[...]
    centred = lifted - jnp.mean(lifted, axis=1, keepdims=True)
    scale = lax.rsqrt(jnp.mean(centred * centred, axis=1, keepdims=True) + 1e-05)
    normed = centred * scale
    normed_f[...] = normed
    c_qkv.wait()
    proj[...] = dot(normed.astype(BF16), w_qkv_v[...]).astype(BF16)
    half = lax.broadcasted_iota(jnp.int32, (TOK, 128), 1) < 64
    zero = jnp.zeros((TOK, 128), BF16)

    def both_heads(pair):
        return jnp.concatenate([jnp.where(half, pair, zero), jnp.where(half, zero, pair)], axis=0)

    def queries(p):
        return both_heads(proj[:, p * 128 : (p + 1) * 128] * 0.125)

    def keys(p):
        return proj[:, features + p * 128 : features + (p + 1) * 128]

    def values(p):
        return proj[:, 2 * features + p * 128 : 2 * features + (p + 1) * 128]

    for p in range(HEADS // 2):
        weights = jnp.exp(dot(keys(p), queries(p), NT)) * allowed
        att[p] = weights * (1.0 / jnp.sum(weights, axis=0, keepdims=True))

    @pl.when(late)
    def _():
        for copy in halo_sends[1]:
            copy.wait_recv()
        for copy in halo_sends[2]:
            copy.start()
        cot_w[...] = dot(pick_halo, ext_halo[1]).astype(BF16)

    @pl.when(jnp.logical_not(late))
    def _():
        pick = one_hot(read_codes(s_early - s_late, t_early - t_late), codes_v[1:2, : mid.padded])
        for copy in mid_sends:
            copy.wait_recv()
        cot_w[...] = dot(pick, ext_mid[...]).astype(BF16)

    c_out.wait()
    d_mixed[...] = dot(cot_w[...], w_out_v[...], NT).astype(BF16)
    for p in range(HEADS // 2):
        d_both = both_heads(d_mixed[:, p * 128 : (p + 1) * 128])
        query, key, attention = queries(p), keys(p), att[p]
        inner = attention * dot(values(p), d_both, NT)
        d_scores = (inner - attention * jnp.sum(inner, axis=0, keepdims=True)).astype(BF16)
        d_query = dot(d_scores, key, TN)
        d_query = jnp.where(half, d_query[:TOK], d_query[TOK:]) * 0.125
        d_proj[:, p * 128 : (p + 1) * 128] = d_query.astype(BF16)
        d_proj[:, features + p * 128 : features + (p + 1) * 128] = dot(d_scores, query).astype(BF16)
        d_proj[:, 2 * features + p * 128 : 2 * features + (p + 1) * 128] = dot(attention.astype(BF16), d_both).astype(BF16)
    d_normed = dot(d_proj[...], w_qkv_v[...], NT).astype(BF16).astype(F32)
    normed = normed_f[...]
    along = jnp.mean(d_normed * normed, axis=1, keepdims=True)
    total = cot_w[...].astype(F32) + scale * (d_normed - jnp.mean(d_normed, axis=1, keepdims=True) - normed * along)
    normed_f[...] = total
    c_pack_out.wait()
    c_pack_mid.wait()

    @pl.when(late)
    def _():
        for copy in halo_sends[2]:
            copy.wait_recv()
        ext_out[pl.ds(0, TOK)] = (normed_f[...] + dot(pick_halo, ext_halo[2])).astype(BF16)
        mid_sends[-1].start()
        send_mid[...] = dot(pack_mid_v[...].astype(BF16), ext_out[pl.ds(0, TOK)]).astype(BF16)
        for copy in mid_sends[:-1]:
            copy.start()

    @pl.when(jnp.logical_not(late))
    def _():
        ext_out[pl.ds(0, TOK)] = normed_f[...].astype(BF16)

    send_out[...] = dot(pack_out_v[...].astype(BF16), ext_out[pl.ds(0, TOK)]).astype(BF16)
    for copy in out_sends:
        copy.start()
    pick_out = one_hot(read_codes(-s, -t), codes_v[2:3, : out.padded])
    for copy in out_sends:
        copy.wait_recv()
    result[...] = dot(pick_out, ext_out[...]).astype(BF16).reshape(result.shape)

    for copy in halo_sends[0] + out_sends:
        copy.wait_send()

    @pl.when(late)
    def _():
        for copy in halo_sends[1] + halo_sends[2] + mid_sends:
            copy.wait_send()


def per_device(sizes, states, final_cot, step_cot, w_qkv, w_out, land_vec, land_sea, ground, shifts):
    halo = Exchange(2, 3, 5, 6)
    mid = Exchange(3, 3, 6, 6)
    out = Exchange(3, 2, 6, 5)
    features = w_qkv.shape[0]
    codes = np.full((8, max(e.padded for e in (halo, mid, out))), -1, np.int32)
    for i, e in enumerate((halo, mid, out)):
        codes[i, : e.padded] = e.codes
    packs = [jnp.asarray(e.pack) for e in (halo, mid, out)]
    any_spec = pl.BlockSpec(memory_space=pl.ANY)

    def field(*shape):
        return pltpu.VMEM(shape, BF16)

    def home(block):
        return jnp.moveaxis(block, 0, 2).reshape(TOK // LEV, LEV, features)

    gradient = pl.pallas_call(
        functools.partial(kernel, sizes, halo, mid, out),
        out_shape=jax.ShapeDtypeStruct((TOK // LEV, LEV, features), BF16),
        in_specs=[any_spec] * 13,
        out_specs=pl.BlockSpec(memory_space=pltpu.VMEM),
        scratch_shapes=[
            field(3, TOK // LEV, LEV, features),
            field(*w_qkv.shape),
            field(*w_out.shape),
            pltpu.VMEM((1, features), F32),
            pltpu.VMEM((2,) + land_sea.shape, jnp.int32),
            pltpu.SMEM(shifts.shape, jnp.int32),
            pltpu.VMEM(halo.pack.shape, F32),
            pltpu.VMEM(mid.pack.shape, F32),
            pltpu.VMEM(out.pack.shape, F32),
            pltpu.VMEM(codes.shape, jnp.int32),
            field(3, halo.padded, features),
            field(mid.padded, features),
            field(out.padded, features),
            field(3, halo.sent, features),
            field(mid.sent, features),
            field(out.sent, features),
            pltpu.VMEM((TOK, features), F32),
            field(TOK, 3 * features),
            pltpu.VMEM((HEADS // 2, TOK, 2 * TOK), F32),
            field(TOK, features),
            field(TOK, 3 * features),
            field(TOK, features),
            pltpu.SemaphoreType.DMA((13,)),
            pltpu.SemaphoreType.DMA((41,)),
            pltpu.SemaphoreType.DMA((41,)),
            pltpu.SemaphoreType.REGULAR,
        ],
        compiler_params=pltpu.CompilerParams(
            collective_id=0, has_side_effects=True, vmem_limit_bytes=60 * 1024 * 1024
        ),
    )(
        home(states[0]), home(final_cot), home(step_cot), w_qkv, w_out, land_vec.reshape(1, features), land_sea, ground, shifts,
        packs[0], packs[1], packs[2], jnp.asarray(codes),
    )
    return jnp.moveaxis(gradient.reshape(WLAT, WLON, LEV, features), 2, 0)[None]


def solution(mesh):
    return jax.shard_map(
        functools.partial(per_device, (mesh.shape["lat"], mesh.shape["lon"])),
        mesh=mesh,
        in_specs=(
            P("step", None, "lat", "lon", None),
            P(None, "lat", "lon", None),
            P(None, "lat", "lon", None),
            P(),
            P(),
            P(),
            P(),
            P(),
            P(),
        ),
        out_specs=P("step", None, "lat", "lon", None),
        check_vma=False,
    )
```

```python
import functools

import jax
import jax.numpy as jnp
import numpy as np
from jax import lax
from jax.experimental import pallas as pl
from jax.experimental.pallas import tpu as pltpu
from jax.sharding import PartitionSpec as P

HEADS = 8
LEV = 2
WLAT = 6
WLON = 12
TOK = WLAT * WLON * LEV
MESH = pl.DeviceIdType.MESH
F32 = jnp.float32
BF16 = jnp.bfloat16
NT = (((1,), (1,)), ((), ()))
TN = (((0,), (0,)), ((), ()))


def up_to(value, unit):
    return -(-value // unit) * unit


class Exchange:
    def __init__(self, first_rows, last_rows, first_cols, last_cols):
        rows = {-1: range(first_rows), 0: range(WLAT), 1: range(WLAT - last_rows, WLAT)}
        cols = {-1: range(first_cols), 0: range(WLON), 1: range(WLON - last_cols, WLON)}
        self.pieces = []
        pack, codes = [], list(range(4 * TOK, 5 * TOK))
        offset = 0
        for dy, dx in ((1, 0), (-1, 0), (0, 1), (0, -1), (1, 1), (1, -1), (-1, 1), (-1, -1)):
            tokens = [(r * WLON + c) * LEV + l for r in rows[dy] for c in cols[dx] for l in range(LEV)]
            if not tokens:
                continue
            size = up_to(len(tokens), 16)
            zone = (1 - dy) * 3 + 1 - dx
            filler = [-1] * (size - len(tokens))
            codes += [zone * TOK + token for token in tokens] + filler
            pack += tokens + filler
            self.pieces.append((dy, dx, offset, size))
            offset += size
        self.sent = offset
        self.rows = TOK + offset
        self.padded = up_to(self.rows, 128)
        self.codes = np.array(codes + [-1] * (self.padded - self.rows), np.int32)
        self.pack = (np.array(pack)[:, None] == np.arange(TOK)[None, :]).astype(np.float32)


def frame_places():
    index = lax.broadcasted_iota(jnp.int32, (TOK, 1), 0)
    place = index >> 1
    row = (place * 43691) >> 19
    return row, place - row * WLON, index & 1


def read_codes(down, right):
    row, col, level = frame_places()
    row_at = row + down
    col_at = col + right
    zone_row = jnp.where(row_at >= WLAT, 1, 0) - jnp.where(row_at < 0, 1, 0)
    zone_col = jnp.where(col_at >= WLON, 1, 0) - jnp.where(col_at < 0, 1, 0)
    place = (row_at - zone_row * WLAT) * WLON + col_at - zone_col * WLON
    return ((zone_row + 1) * 3 + zone_col + 1) * TOK + place * LEV + level


def one_hot(left, right):
    return jnp.where(left == right, 1.0, 0.0).astype(BF16)


def dot(a, b, dims=(((1,), (0,)), ((), ()))):
    return lax.dot_general(a, b, dims, preferred_element_type=F32)


def kernel(
    sizes, starts, halo, mid, out,
    states, final_cot, step_cot, w_qkv, w_out, land_vec, land_sea, ground, shifts,
    pack_halo, pack_mid, pack_out, codes,
    result,
    raw, w_qkv_v, w_out_v, land_vec_v, tables_v, shifts_v, pack_halo_v, pack_mid_v, pack_out_v, codes_v,
    ext_halo, ext_mid, ext_out, send_halo, send_mid, send_out,
    normed_f, proj, att, cot_w, d_proj, d_mixed,
    local_sem, send_sem, recv_sem, go_sem,
):
    n_lat, n_lon = sizes
    features = raw.shape[-1]
    step, lat, lon = lax.axis_index("step"), lax.axis_index("lat"), lax.axis_index("lon")
    late = step == 1

    def around(dy, dx, other=False):
        return (
            1 - step if other else step,
            lax.rem(lat + (dy + n_lat), n_lat),
            lax.rem(lon + (dx + n_lon), n_lon),
        )

    barrier = pltpu.get_barrier_semaphore()
    for dy in (-1, 0, 1):
        for dx in (-1, 0, 1):
            if (dy, dx) != (0, 0):
                pl.semaphore_signal(barrier, inc=1, device_id=around(dy, dx), device_id_type=MESH)
            pl.semaphore_signal(barrier, inc=1, device_id=around(dy, dx, True), device_id_type=MESH)

    local = [
        pltpu.make_async_copy(src, dst, local_sem.at[i])
        for i, (src, dst) in enumerate((
            (states, raw.at[0]),
            (pack_halo, pack_halo_v),
            (final_cot, raw.at[1]),
            (step_cot, raw.at[2]),
            (shifts, shifts_v),
            (codes, codes_v),
            (land_sea, tables_v.at[0]),
            (ground, tables_v.at[1]),
            (land_vec, land_vec_v),
            (w_qkv, w_qkv_v),
            (w_out, w_out_v),
            (pack_out, pack_out_v),
            (pack_mid, pack_mid_v),
        ))
    ]
    (c_state, c_pack, c_final, c_step, c_shift, c_codes, c_land, c_ground, c_vec, c_qkv, c_out, c_pack_out, c_pack_mid) = local
    for copy in local:
        copy.start()

    def sends(which, exchange, buffer, target, other=False):
        made = []
        base = (0, 8, 16, 24, 32)[which]
        for k, (dy, dx, offset, size) in enumerate(exchange.pieces):
            made.append(pltpu.make_async_remote_copy(
                src_ref=buffer.at[pl.ds(offset, size)],
                dst_ref=target.at[pl.ds(TOK + offset, size)],
                send_sem=send_sem.at[base + k],
                recv_sem=recv_sem.at[base + k],
                device_id=around(dy, dx, other),
                device_id_type=MESH,
            ))
        return made

    halo_sends = [[sends(i, halo[half], send_halo.at[i], ext_halo.at[i]) for i in range(1 + 2 * half)] for half in range(2)]
    mid_sends = sends(3, mid, send_mid, ext_mid, True)
    mid_sends.append(pltpu.make_async_remote_copy(
        src_ref=ext_out.at[pl.ds(0, TOK)],
        dst_ref=ext_mid.at[pl.ds(0, TOK)],
        send_sem=send_sem.at[40],
        recv_sem=recv_sem.at[40],
        device_id=around(0, 0, True),
        device_id_type=MESH,
    ))
    out_sends = [sends(4, out[half], send_out, ext_out) for half in range(2)]

    def pack_field(i):
        field = raw[i].reshape(TOK, features)
        ext_halo[i, pl.ds(0, TOK)] = field
        send_halo[i] = dot(pack_halo_v[step].astype(BF16), field).astype(BF16)

    def clear(target, exchange):
        rows = target.shape[0] - exchange.rows
        if rows:
            target[pl.ds(exchange.rows, rows)] = jnp.zeros((rows, features), BF16)

    @pl.when(late)
    def _():
        for i in range(3):
            clear(ext_halo.at[i], halo[1])
        clear(ext_out, out[1])

    @pl.when(jnp.logical_not(late))
    def _():
        clear(ext_halo.at[0], halo[0])
        clear(ext_mid, mid)
        clear(ext_out, out[0])

    c_state.wait()
    c_pack.wait()
    pack_field(0)
    pl.semaphore_wait(barrier, 17)

    c_final.wait()
    c_step.wait()

    @pl.when(late)
    def _():
        for copy in halo_sends[1][0]:
            copy.start()
        pack_field(1)
        for copy in halo_sends[1][1]:
            copy.start()
        pack_field(2)

    c_shift.wait()
    s_early, s_late = starts
    t_early, t_late = (jnp.where(b >= 6, b - WLON, b) for b in (shifts_v[0, 1], shifts_v[1, 1]))
    s = jnp.where(late, s_late, s_early)
    t = jnp.where(late, t_late, t_early)
    c_codes.wait()
    pick_halo = one_hot(read_codes(s, t), jnp.where(late, codes_v[1:2, : ext_halo.shape[1]], codes_v[0:1, : ext_halo.shape[1]]))

    row, col, level = frame_places()
    lat_total, lon_total = tables_v.shape[1], tables_v.shape[2]
    at_row = lat * WLAT + s + row
    at_row = jnp.where(at_row < 0, at_row + lat_total, jnp.where(at_row >= lat_total, at_row - lat_total, at_row))
    at_col = lon * WLON + t + col
    at_col = jnp.where(at_col < 0, at_col + lon_total, jnp.where(at_col >= lon_total, at_col - lon_total, at_col))
    c_land.wait()
    c_ground.wait()
    row_pick = one_hot(at_row, lax.broadcasted_iota(jnp.int32, (TOK, lat_total), 1))
    col_pick = at_col == lax.broadcasted_iota(jnp.int32, (TOK, lon_total), 1)

    def looked_up(i):
        lines = dot(row_pick, tables_v[i].astype(F32).astype(BF16))
        return jnp.sum(jnp.where(col_pick, lines, 0.0), axis=1, keepdims=True)

    land = looked_up(0)
    key_valid = jnp.where(level.astype(F32) >= looked_up(1), 1.0, 0.0)
    shift_lat = jnp.where(s < 0, s + WLAT, s)
    window = jnp.where(s < 0, lax.rem(lat + (n_lat - 1), n_lat), lat)
    first_seam = jnp.where(window == n_lat - 1, WLAT - shift_lat, WLAT)
    lane = lax.broadcasted_iota(jnp.int32, (1, 2 * TOK), 1)
    lane = jnp.where(lane >= TOK, lane - TOK, lane)
    lane_row = ((lane >> 1) * 43691) >> 19
    seam_key = jnp.where(row >= first_seam, 1, 0)
    seam_query = jnp.where(lane_row >= first_seam, 1, 0)
    allowed = jnp.where(seam_key == seam_query, key_valid, 0.0)
    c_vec.wait()

    @pl.when(late)
    def _():
        for copy in halo_sends[1][0]:
            copy.wait_recv()
        pl.semaphore_signal(go_sem, inc=1, device_id=around(0, 0, True), device_id_type=MESH)

    @pl.when(jnp.logical_not(late))
    def _():
        pl.semaphore_wait(go_sem, 1)
        for copy in halo_sends[0][0]:
            copy.start()
        for copy in halo_sends[0][0]:
            copy.wait_recv()

    lifted = dot(pick_halo, ext_halo[0]) + land * land_vec_v[...]
    centred = lifted - jnp.mean(lifted, axis=1, keepdims=True)
    scale = lax.rsqrt(jnp.mean(centred * centred, axis=1, keepdims=True) + 1e-05)
    normed = centred * scale
    normed_f[...] = normed
    c_qkv.wait()
    proj[...] = dot(normed.astype(BF16), w_qkv_v[...]).astype(BF16)
    half = lax.broadcasted_iota(jnp.int32, (TOK, 128), 1) < 64
    zero = jnp.zeros((TOK, 128), BF16)

    def both_heads(pair):
        return jnp.concatenate([jnp.where(half, pair, zero), jnp.where(half, zero, pair)], axis=0)

    def queries(p):
        return both_heads(proj[:, p * 128 : (p + 1) * 128] * 0.125)

    def keys(p):
        return proj[:, features + p * 128 : features + (p + 1) * 128]

    def values(p):
        return proj[:, 2 * features + p * 128 : 2 * features + (p + 1) * 128]

    for p in range(HEADS // 2):
        weights = jnp.exp(dot(keys(p), queries(p), NT)) * allowed
        att[p] = weights * (1.0 / jnp.sum(weights, axis=0, keepdims=True))

    @pl.when(late)
    def _():
        for copy in halo_sends[1][1]:
            copy.wait_recv()
        for copy in halo_sends[1][2]:
            copy.start()
        cot_w[...] = dot(pick_halo, ext_halo[1]).astype(BF16)

    @pl.when(jnp.logical_not(late))
    def _():
        pick = one_hot(read_codes(s_early - s_late, t_early - t_late), codes_v[4:5, : mid.padded])
        for copy in mid_sends:
            copy.wait_recv()
        cot_w[...] = dot(pick, ext_mid[...]).astype(BF16)

    c_out.wait()
    d_mixed[...] = dot(cot_w[...], w_out_v[...], NT).astype(BF16)
    for p in range(HEADS // 2):
        d_both = both_heads(d_mixed[:, p * 128 : (p + 1) * 128])
        query, key, attention = queries(p), keys(p), att[p]
        inner = attention * dot(values(p), d_both, NT)
        d_scores = (inner - attention * jnp.sum(inner, axis=0, keepdims=True)).astype(BF16)
        d_query = dot(d_scores, key, TN)
        d_query = jnp.where(half, d_query[:TOK], d_query[TOK:]) * 0.125
        d_proj[:, p * 128 : (p + 1) * 128] = d_query.astype(BF16)
        d_proj[:, features + p * 128 : features + (p + 1) * 128] = dot(d_scores, query).astype(BF16)
        d_proj[:, 2 * features + p * 128 : 2 * features + (p + 1) * 128] = dot(attention.astype(BF16), d_both).astype(BF16)
    d_normed = dot(d_proj[...], w_qkv_v[...], NT).astype(BF16).astype(F32)
    normed = normed_f[...]
    along = jnp.mean(d_normed * normed, axis=1, keepdims=True)
    total = cot_w[...].astype(F32) + scale * (d_normed - jnp.mean(d_normed, axis=1, keepdims=True) - normed * along)
    normed_f[...] = total
    c_pack_out.wait()
    c_pack_mid.wait()

    @pl.when(late)
    def _():
        for copy in halo_sends[1][2]:
            copy.wait_recv()
        ext_out[pl.ds(0, TOK)] = (normed_f[...] + dot(pick_halo, ext_halo[2])).astype(BF16)
        mid_sends[-1].start()
        send_mid[...] = dot(pack_mid_v[...].astype(BF16), ext_out[pl.ds(0, TOK)]).astype(BF16)
        for copy in mid_sends[:-1]:
            copy.start()

    @pl.when(jnp.logical_not(late))
    def _():
        ext_out[pl.ds(0, TOK)] = normed_f[...].astype(BF16)

    send_out[...] = dot(pack_out_v[step].astype(BF16), ext_out[pl.ds(0, TOK)]).astype(BF16)

    @pl.when(late)
    def _():
        for copy in out_sends[1]:
            copy.start()

    @pl.when(jnp.logical_not(late))
    def _():
        for copy in out_sends[0]:
            copy.start()

    rows = ext_out.shape[0]
    pick_out = one_hot(read_codes(-s, -t), jnp.where(late, codes_v[3:4, :rows], codes_v[2:3, :rows]))

    @pl.when(late)
    def _():
        for copy in out_sends[1]:
            copy.wait_recv()

    @pl.when(jnp.logical_not(late))
    def _():
        for copy in out_sends[0]:
            copy.wait_recv()

    result[...] = dot(pick_out, ext_out[...]).astype(BF16).reshape(result.shape)

    @pl.when(late)
    def _():
        for copy in halo_sends[1][0] + halo_sends[1][1] + halo_sends[1][2] + mid_sends + out_sends[1]:
            copy.wait_send()

    @pl.when(jnp.logical_not(late))
    def _():
        for copy in halo_sends[0][0] + out_sends[0]:
            copy.wait_send()


def variant(sizes, number, starts, states, final_cot, step_cot, w_qkv, w_out, land_vec, land_sea, ground, shifts):
    down = [max(start, 0) for start in starts]
    up = [max(-start, 0) for start in starts]
    apart = starts[0] - starts[1]
    halo = [Exchange(down[half], up[half], 5, 6) for half in range(2)]
    mid = Exchange(max(apart, 0), max(-apart, 0), 6, 6)
    out = [Exchange(up[half], down[half], 6, 5) for half in range(2)]
    features = w_qkv.shape[0]
    exchanges = halo + out + [mid]
    codes = np.full((8, max(e.padded for e in exchanges)), -1, np.int32)
    for i, e in enumerate(exchanges):
        codes[i, : e.padded] = e.codes

    def packed(pair):
        packs = np.zeros((2, max(e.sent for e in pair), TOK), np.float32)
        for half, e in enumerate(pair):
            packs[half, : e.sent] = e.pack
        return packs

    packs = [packed(halo), mid.pack, packed(out)]
    rows_halo = max(e.padded for e in halo)
    rows_out = max(e.padded for e in out)
    any_spec = pl.BlockSpec(memory_space=pl.ANY)

    def field(*shape):
        return pltpu.VMEM(shape, BF16)

    def home(block):
        return jnp.moveaxis(block, 0, 2).reshape(TOK // LEV, LEV, features)

    gradient = pl.pallas_call(
        functools.partial(kernel, sizes, starts, halo, mid, out),
        out_shape=jax.ShapeDtypeStruct((TOK // LEV, LEV, features), BF16),
        in_specs=[any_spec] * 13,
        out_specs=pl.BlockSpec(memory_space=pltpu.VMEM),
        scratch_shapes=[
            field(3, TOK // LEV, LEV, features),
            field(*w_qkv.shape),
            field(*w_out.shape),
            pltpu.VMEM((1, features), F32),
            pltpu.VMEM((2,) + land_sea.shape, jnp.int32),
            pltpu.SMEM(shifts.shape, jnp.int32),
            pltpu.VMEM(packs[0].shape, F32),
            pltpu.VMEM(packs[1].shape, F32),
            pltpu.VMEM(packs[2].shape, F32),
            pltpu.VMEM(codes.shape, jnp.int32),
            field(3, rows_halo, features),
            field(mid.padded, features),
            field(rows_out, features),
            field(3, packs[0].shape[1], features),
            field(mid.sent, features),
            field(packs[2].shape[1], features),
            pltpu.VMEM((TOK, features), F32),
            field(TOK, 3 * features),
            pltpu.VMEM((HEADS // 2, TOK, 2 * TOK), F32),
            field(TOK, features),
            field(TOK, 3 * features),
            field(TOK, features),
            pltpu.SemaphoreType.DMA((13,)),
            pltpu.SemaphoreType.DMA((41,)),
            pltpu.SemaphoreType.DMA((41,)),
            pltpu.SemaphoreType.REGULAR,
        ],
        compiler_params=pltpu.CompilerParams(
            collective_id=number, has_side_effects=True, vmem_limit_bytes=60 * 1024 * 1024
        ),
    )(
        home(states[0]), home(final_cot), home(step_cot), w_qkv, w_out, land_vec.reshape(1, features), land_sea, ground, shifts,
        *(jnp.asarray(pack) for pack in packs), jnp.asarray(codes),
    )
    return jnp.moveaxis(gradient.reshape(WLAT, WLON, LEV, features), 2, 0)[None]


def per_device(sizes, *operands):
    others = (1, 2, 3 - WLAT, 4 - WLAT, -1)
    pairs = [(start, -1) for start in others] + [(-1, start) for start in others[:-1]]
    shifts = operands[-1]
    case = jnp.where(shifts[1, 0] == 5, shifts[0, 0] - 1, shifts[1, 0] + 4)
    cases = [functools.partial(variant, sizes, number, pair) for number, pair in enumerate(pairs)]
    return lax.switch(case, cases, *operands)


def solution(mesh):
    return jax.shard_map(
        functools.partial(per_device, (mesh.shape["lat"], mesh.shape["lon"])),
        mesh=mesh,
        in_specs=(
            P("step", None, "lat", "lon", None),
            P(None, "lat", "lon", None),
            P(None, "lat", "lon", None),
            P(),
            P(),
            P(),
            P(),
            P(),
            P(),
        ),
        out_specs=P("step", None, "lat", "lon", None),
        check_vma=False,
    )
```

```python
import functools

import jax
import jax.numpy as jnp
import numpy as np
from jax import lax
from jax.experimental import pallas as pl
from jax.experimental.pallas import tpu as pltpu
from jax.sharding import PartitionSpec as P

HEADS = 8
LEV = 2
WLAT = 6
WLON = 12
ROW = WLON * LEV
TOK = WLAT * ROW
LON_CODE = 1000
MESH = pl.DeviceIdType.MESH
F32 = jnp.float32
BF16 = jnp.bfloat16
NT = (((1,), (1,)), ((), ()))
TN = (((0,), (0,)), ((), ()))


def up_to(value, unit):
    return -(-value // unit) * unit


class Exchange:
    def __init__(self, first_rows, last_rows, first_cols, last_cols):
        self.first_cols, self.last_cols = first_cols, last_cols
        self.tail = (WLAT - last_rows) * ROW // 16 * 16
        self.from_before = TOK - self.tail
        self.from_after = up_to(first_rows * ROW, 16)
        self.rows_held = TOK + self.from_before + self.from_after
        self.cols_last = up_to(WLAT * last_cols * LEV, 16)
        self.cols_first = up_to(WLAT * first_cols * LEV, 16)
        self.cols_sent = self.cols_last + self.cols_first
        self.held = self.rows_held + self.cols_sent
        codes = [TOK + token for token in range(TOK)]
        codes += [token for token in range(self.tail, TOK)]
        codes += [2 * TOK + token for token in range(self.from_after)]
        for size, cols in (
            (self.cols_last, range(-last_cols, 0)),
            (self.cols_first, range(WLON, WLON + first_cols)),
        ):
            came = [LON_CODE + (r * 36 + c + WLON) * LEV + l for r in range(WLAT) for c in cols for l in range(LEV)]
            codes += came + [-1] * (size - len(came))
        self.codes = np.array(codes, np.int32)

    def sent_codes(self, down):
        index = lax.broadcasted_iota(jnp.int32, (self.cols_sent, 1), 0)
        is_last = index < self.cols_last
        index = jnp.where(is_last, index, index - self.cols_last)
        place = index >> 1
        row_last, row_first = quotient(place, self.last_cols), quotient(place, self.first_cols)
        row = jnp.where(is_last, row_last, row_first)
        col = place - jnp.where(is_last, row_last * self.last_cols - (WLON - self.last_cols), row_first * self.first_cols)
        return jnp.where(row < WLAT, ROW * (row + down + WLAT) + LEV * col + (index & 1), -2)


def quotient(value, by):
    factor = (1 << 14) // by + 1
    assert all((i * factor) >> 14 == i // by for i in range(TOK + 1))
    return (value * factor) >> 14


def frame_places():
    index = lax.broadcasted_iota(jnp.int32, (TOK, 1), 0)
    place = index >> 1
    row = quotient(place, WLON)
    return row, place - row * WLON, index & 1


def read_codes(down, right):
    row, col, level = frame_places()
    col = col + right
    with_rows = ROW * (row + down + WLAT) + LEV * col + level
    with_cols = LON_CODE + (row * 36 + col + WLON) * LEV + level
    return jnp.where((col >= 0) & (col < WLON), with_rows, with_cols)


def one_hot(left, right):
    return jnp.where(left == right, 1.0, 0.0).astype(BF16)


def dot(a, b, dims=(((1,), (0,)), ((), ()))):
    return lax.dot_general(a, b, dims, preferred_element_type=F32)


def kernel(
    sizes, halo, mid, out,
    states, final_cot, step_cot, w_qkv, w_out, land_vec, land_sea, ground, shifts, codes,
    result,
    raw, w_qkv_v, w_out_v, land_vec_v, tables_v, shifts_v, codes_v,
    ext_halo, ext_mid, ext_out, send_cols, pick_halo, pick_cols,
    normed_f, proj, att, cot_w, d_proj, d_mixed,
    local_sem, send_sem, recv_sem, go_sem,
):
    n_lat, n_lon = sizes
    features = raw.shape[-1]
    step, lat, lon = lax.axis_index("step"), lax.axis_index("lat"), lax.axis_index("lon")
    late = step == 1
    early = step == 0

    def around(dy, dx, other=False):
        return (
            1 - step if other else step,
            lax.rem(lat + (dy + n_lat), n_lat),
            lax.rem(lon + (dx + n_lon), n_lon),
        )

    barrier = pltpu.get_barrier_semaphore()
    partners = [(1, 0), (-1, 0), (0, 1), (0, -1), (0, 0, True), (1, 0, True), (-1, 0, True)]
    for partner in partners:
        pl.semaphore_signal(barrier, inc=1, device_id=around(*partner), device_id_type=MESH)

    local = [
        pltpu.make_async_copy(src, dst, local_sem.at[i])
        for i, (src, dst) in enumerate((
            (states, raw.at[0]),
            (final_cot, raw.at[1]),
            (step_cot, raw.at[2]),
            (shifts, shifts_v),
            (codes, codes_v),
            (land_sea, tables_v.at[0]),
            (ground, tables_v.at[1]),
            (land_vec, land_vec_v),
            (w_qkv, w_qkv_v),
            (w_out, w_out_v),
        ))
    ]
    (c_state, c_final, c_step, c_shift, c_codes, c_land, c_ground, c_vec, c_qkv, c_out) = local
    for copy in local:
        copy.start()

    def remote(slot, src, dst, to):
        return pltpu.make_async_remote_copy(
            src_ref=src, dst_ref=dst, send_sem=send_sem.at[slot], recv_sem=recv_sem.at[slot],
            device_id=around(*to), device_id_type=MESH,
        )

    def row_sends(which, exchange, held, other=False, target=None):
        target = held if target is None else target
        return [
            remote(
                4 * which, held.at[pl.ds(exchange.tail, exchange.from_before)],
                target.at[pl.ds(TOK, exchange.from_before)], (1, 0, other),
            ),
            remote(
                4 * which + 1, held.at[pl.ds(0, exchange.from_after)],
                target.at[pl.ds(TOK + exchange.from_before, exchange.from_after)], (-1, 0, other),
            ),
        ]

    def col_sends(which, exchange, held):
        packed = send_cols.at[which]
        return [
            remote(
                4 * which + 2, packed.at[pl.ds(0, exchange.cols_last)],
                held.at[pl.ds(exchange.rows_held, exchange.cols_last)], (0, 1),
            ),
            remote(
                4 * which + 3, packed.at[pl.ds(exchange.cols_last, exchange.cols_first)],
                held.at[pl.ds(exchange.rows_held + exchange.cols_last, exchange.cols_first)], (0, -1),
            ),
        ]

    def started(copies):
        for copy in copies:
            copy.start()

    def arrived(copies):
        for copy in copies:
            copy.wait_recv()

    halo_rows = [row_sends(i, halo, ext_halo.at[i]) for i in range(3)]
    halo_cols = [col_sends(i, halo, ext_halo.at[i]) for i in range(3)]
    mid_rows = row_sends(3, mid, ext_out, True, ext_mid)
    mid_rows.append(remote(20, ext_out.at[pl.ds(0, TOK)], ext_mid.at[pl.ds(0, TOK)], (0, 0, True)))
    mid_cols = col_sends(3, mid, ext_mid)
    out_rows = row_sends(4, out, ext_out)
    out_cols = col_sends(4, out, ext_out)

    def forward_cols(which, exchange, held, picked):
        rows = dot(picked, held[pl.ds(0, exchange.rows_held)])
        send_cols[which, pl.ds(0, exchange.cols_sent)] = rows.astype(BF16)

    c_state.wait()
    ext_halo[0, pl.ds(0, TOK)] = raw[0].reshape(TOK, features)
    c_final.wait()
    c_step.wait()

    @pl.when(late)
    def _():
        ext_halo[1, pl.ds(0, TOK)] = raw[1].reshape(TOK, features)
        ext_halo[2, pl.ds(0, TOK)] = raw[2].reshape(TOK, features)

    pl.semaphore_wait(barrier, len(partners))

    @pl.when(late)
    def _():
        started(halo_rows[0] + halo_rows[1] + halo_rows[2])

    c_shift.wait()

    def start_of(row):
        a, b = shifts_v[row, 0], shifts_v[row, 1]
        return jnp.where(a >= 3, a - WLAT, a), jnp.where(b >= 6, b - WLON, b)

    s_late, t_late = start_of(1)
    s_early, t_early = start_of(0)
    s = jnp.where(late, s_late, s_early)
    t = jnp.where(late, t_late, t_early)
    c_codes.wait()
    pick_cols[...] = one_hot(halo.sent_codes(s), codes_v[0:1, : halo.rows_held])
    pick_halo[...] = one_hot(read_codes(s, t), codes_v[0:1, : halo.held])

    row, col, level = frame_places()
    lat_total, lon_total = tables_v.shape[1], tables_v.shape[2]
    at_row = lat * WLAT + s + row
    at_row = jnp.where(at_row < 0, at_row + lat_total, jnp.where(at_row >= lat_total, at_row - lat_total, at_row))
    at_col = lon * WLON + t + col
    at_col = jnp.where(at_col < 0, at_col + lon_total, jnp.where(at_col >= lon_total, at_col - lon_total, at_col))
    c_land.wait()
    c_ground.wait()
    row_pick = one_hot(at_row, lax.broadcasted_iota(jnp.int32, (TOK, lat_total), 1))
    col_pick = at_col == lax.broadcasted_iota(jnp.int32, (TOK, lon_total), 1)

    def looked_up(i):
        lines = dot(row_pick, tables_v[i].astype(F32).astype(BF16))
        return jnp.sum(jnp.where(col_pick, lines, 0.0), axis=1, keepdims=True)

    land = looked_up(0)
    key_valid = jnp.where(level.astype(F32) >= looked_up(1), 1.0, 0.0)
    shift_lat = jnp.where(s < 0, s + WLAT, s)
    window = jnp.where(s < 0, lax.rem(lat + (n_lat - 1), n_lat), lat)
    first_seam = jnp.where(window == n_lat - 1, WLAT - shift_lat, WLAT)
    lane = lax.broadcasted_iota(jnp.int32, (1, 2 * TOK), 1)
    lane = jnp.where(lane >= TOK, lane - TOK, lane)
    seam_key = jnp.where(row >= first_seam, 1, 0)
    seam_query = jnp.where(quotient(lane >> 1, WLON) >= first_seam, 1, 0)
    allowed = jnp.where(seam_key == seam_query, key_valid, 0.0)
    c_vec.wait()

    @pl.when(early)
    def _():
        pl.semaphore_wait(go_sem, 1)
        started(halo_rows[0])

    arrived(halo_rows[0])
    forward_cols(0, halo, ext_halo.at[0], pick_cols[...])
    started(halo_cols[0])

    @pl.when(late)
    def _():
        arrived(halo_rows[1])
        pl.semaphore_signal(go_sem, inc=1, device_id=around(0, 0, True), device_id_type=MESH)
        forward_cols(1, halo, ext_halo.at[1], pick_cols[...])
        started(halo_cols[1])

    arrived(halo_cols[0])

    lifted = dot(pick_halo[...], ext_halo[0]) + land * land_vec_v[...]
    centred = lifted - jnp.mean(lifted, axis=1, keepdims=True)
    scale = lax.rsqrt(jnp.mean(centred * centred, axis=1, keepdims=True) + 1e-05)
    normed = centred * scale
    normed_f[...] = normed
    c_qkv.wait()
    proj[...] = dot(normed.astype(BF16), w_qkv_v[...]).astype(BF16)
    half = lax.broadcasted_iota(jnp.int32, (TOK, 128), 1) < 64
    zero = jnp.zeros((TOK, 128), BF16)

    def both_heads(pair):
        return jnp.concatenate([jnp.where(half, pair, zero), jnp.where(half, zero, pair)], axis=0)

    def queries(p):
        return both_heads(proj[:, p * 128 : (p + 1) * 128] * 0.125)

    def keys(p):
        return proj[:, features + p * 128 : features + (p + 1) * 128]

    def values(p):
        return proj[:, 2 * features + p * 128 : 2 * features + (p + 1) * 128]

    for p in range(HEADS // 2):
        weights = jnp.exp(dot(keys(p), queries(p), NT)) * allowed
        att[p] = weights * (1.0 / jnp.sum(weights, axis=0, keepdims=True))

    @pl.when(late)
    def _():
        arrived(halo_rows[2])
        forward_cols(2, halo, ext_halo.at[2], pick_cols[...])
        started(halo_cols[2])
        arrived(halo_cols[1])
        cot_w[...] = dot(pick_halo[...], ext_halo[1]).astype(BF16)

    @pl.when(early)
    def _():
        down, right = s_early - s_late, t_early - t_late
        picked = one_hot(mid.sent_codes(down), codes_v[1:2, : mid.rows_held])
        pick = one_hot(read_codes(down, right), codes_v[1:2, : mid.held])
        arrived(mid_rows)
        forward_cols(3, mid, ext_mid, picked)
        started(mid_cols)
        arrived(mid_cols)
        cot_w[...] = dot(pick, ext_mid[...]).astype(BF16)

    c_out.wait()
    d_mixed[...] = dot(cot_w[...], w_out_v[...], NT).astype(BF16)
    for p in range(HEADS // 2):
        d_both = both_heads(d_mixed[:, p * 128 : (p + 1) * 128])
        query, key, attention = queries(p), keys(p), att[p]
        inner = attention * dot(values(p), d_both, NT)
        d_scores = (inner - attention * jnp.sum(inner, axis=0, keepdims=True)).astype(BF16)
        d_query = dot(d_scores, key, TN)
        d_query = jnp.where(half, d_query[:TOK], d_query[TOK:]) * 0.125
        d_proj[:, p * 128 : (p + 1) * 128] = d_query.astype(BF16)
        d_proj[:, features + p * 128 : features + (p + 1) * 128] = dot(d_scores, query).astype(BF16)
        d_proj[:, 2 * features + p * 128 : 2 * features + (p + 1) * 128] = dot(attention.astype(BF16), d_both).astype(BF16)
    d_normed = dot(d_proj[...], w_qkv_v[...], NT).astype(BF16).astype(F32)
    normed = normed_f[...]
    along = jnp.mean(d_normed * normed, axis=1, keepdims=True)
    total = cot_w[...].astype(F32) + scale * (d_normed - jnp.mean(d_normed, axis=1, keepdims=True) - normed * along)
    normed_f[...] = total

    @pl.when(late)
    def _():
        arrived(halo_cols[2])
        ext_out[pl.ds(0, TOK)] = (normed_f[...] + dot(pick_halo[...], ext_halo[2])).astype(BF16)
        started(mid_rows)

    @pl.when(early)
    def _():
        ext_out[pl.ds(0, TOK)] = normed_f[...].astype(BF16)

    started(out_rows)
    picked = one_hot(out.sent_codes(-s), codes_v[2:3, : out.rows_held])
    pick_out = one_hot(read_codes(-s, -t), codes_v[2:3, : out.held])
    arrived(out_rows)
    forward_cols(4, out, ext_out, picked)
    started(out_cols)
    arrived(out_cols)
    result[...] = dot(pick_out, ext_out[...]).astype(BF16).reshape(result.shape)

    for copy in halo_rows[0] + halo_cols[0] + out_rows + out_cols:
        copy.wait_send()

    @pl.when(late)
    def _():
        for copy in halo_rows[1] + halo_cols[1] + halo_rows[2] + halo_cols[2] + mid_rows:
            copy.wait_send()

    @pl.when(early)
    def _():
        for copy in mid_cols:
            copy.wait_send()


def per_device(sizes, states, final_cot, step_cot, w_qkv, w_out, land_vec, land_sea, ground, shifts):
    halo = Exchange(2, 3, 5, 6)
    mid = Exchange(3, 3, 6, 6)
    out = Exchange(3, 2, 6, 5)
    features = w_qkv.shape[0]
    codes = np.full((8, 512), -1, np.int32)
    for i, e in enumerate((halo, mid, out)):
        codes[i, : e.held] = e.codes
    any_spec = pl.BlockSpec(memory_space=pl.ANY)

    def field(*shape):
        return pltpu.VMEM(shape, BF16)

    def home(block):
        return jnp.moveaxis(block, 0, 2).reshape(TOK // LEV, LEV, features)

    gradient = pl.pallas_call(
        functools.partial(kernel, sizes, halo, mid, out),
        out_shape=jax.ShapeDtypeStruct((TOK // LEV, LEV, features), BF16),
        in_specs=[any_spec] * 10,
        out_specs=pl.BlockSpec(memory_space=pltpu.VMEM),
        scratch_shapes=[
            field(3, TOK // LEV, LEV, features),
            field(*w_qkv.shape),
            field(*w_out.shape),
            pltpu.VMEM((1, features), F32),
            pltpu.VMEM((2,) + land_sea.shape, jnp.int32),
            pltpu.SMEM(shifts.shape, jnp.int32),
            pltpu.VMEM(codes.shape, jnp.int32),
            field(3, halo.held, features),
            field(mid.held, features),
            field(out.held, features),
            field(5, max(e.cols_sent for e in (halo, mid, out)), features),
            field(TOK, halo.held),
            field(halo.cols_sent, halo.rows_held),
            pltpu.VMEM((TOK, features), F32),
            field(TOK, 3 * features),
            pltpu.VMEM((HEADS // 2, TOK, 2 * TOK), F32),
            field(TOK, features),
            field(TOK, 3 * features),
            field(TOK, features),
            pltpu.SemaphoreType.DMA((10,)),
            pltpu.SemaphoreType.DMA((21,)),
            pltpu.SemaphoreType.DMA((21,)),
            pltpu.SemaphoreType.REGULAR,
        ],
        compiler_params=pltpu.CompilerParams(
            collective_id=0, has_side_effects=True, vmem_limit_bytes=60 * 1024 * 1024
        ),
    )(
        home(states[0]), home(final_cot), home(step_cot), w_qkv, w_out, land_vec.reshape(1, features),
        land_sea, ground, shifts, jnp.asarray(codes),
    )
    return jnp.moveaxis(gradient.reshape(WLAT, WLON, LEV, features), 2, 0)[None]


def solution(mesh):
    return jax.shard_map(
        functools.partial(per_device, (mesh.shape["lat"], mesh.shape["lon"])),
        mesh=mesh,
        in_specs=(
            P("step", None, "lat", "lon", None),
            P(None, "lat", "lon", None),
            P(None, "lat", "lon", None),
            P(),
            P(),
            P(),
            P(),
            P(),
            P(),
        ),
        out_specs=P("step", None, "lat", "lon", None),
        check_vma=False,
    )
```

```python
import functools

import jax
import jax.numpy as jnp
import numpy as np
from jax import lax
from jax.experimental import pallas as pl
from jax.experimental.pallas import tpu as pltpu
from jax.sharding import PartitionSpec as P

HEADS = 8
LEV = 2
WLAT = 6
WLON = 12
ROW = WLON * LEV
TOK = WLAT * ROW
LON_CODE = 1000
MESH = pl.DeviceIdType.MESH
F32 = jnp.float32
BF16 = jnp.bfloat16
NT = (((1,), (1,)), ((), ()))
TN = (((0,), (0,)), ((), ()))


def up_to(value, unit):
    return -(-value // unit) * unit


class Exchange:
    def __init__(self, first_rows, last_rows, first_cols, last_cols):
        self.first_cols, self.last_cols = first_cols, last_cols
        self.tail = (WLAT - last_rows) * ROW // 16 * 16
        self.from_before = TOK - self.tail
        self.from_after = up_to(first_rows * ROW, 16)
        self.rows_held = TOK + self.from_before + self.from_after
        self.cols_last = up_to(WLAT * last_cols * LEV, 16)
        self.cols_first = up_to(WLAT * first_cols * LEV, 16)
        self.cols_sent = self.cols_last + self.cols_first
        self.held = self.rows_held + self.cols_sent
        codes = [TOK + token for token in range(TOK)]
        codes += [token for token in range(self.tail, TOK)]
        codes += [2 * TOK + token for token in range(self.from_after)]
        for size, cols in (
            (self.cols_last, range(-last_cols, 0)),
            (self.cols_first, range(WLON, WLON + first_cols)),
        ):
            came = [LON_CODE + (r * 36 + c + WLON) * LEV + l for r in range(WLAT) for c in cols for l in range(LEV)]
            codes += came + [-1] * (size - len(came))
        self.codes = np.array(codes, np.int32)

    def sent_codes(self, down):
        index = lax.broadcasted_iota(jnp.int32, (self.cols_sent, 1), 0)
        is_last = index < self.cols_last
        index = jnp.where(is_last, index, index - self.cols_last)
        place = index >> 1
        row_last, row_first = quotient(place, self.last_cols), quotient(place, self.first_cols)
        row = jnp.where(is_last, row_last, row_first)
        col = place - jnp.where(is_last, row_last * self.last_cols - (WLON - self.last_cols), row_first * self.first_cols)
        return jnp.where(row < WLAT, ROW * (row + down + WLAT) + LEV * col + (index & 1), -2)


def quotient(value, by):
    factor = (1 << 14) // by + 1
    assert all((i * factor) >> 14 == i // by for i in range(TOK + 1))
    return (value * factor) >> 14


def frame_places():
    index = lax.broadcasted_iota(jnp.int32, (TOK, 1), 0)
    place = index >> 1
    row = quotient(place, WLON)
    return row, place - row * WLON, index & 1


def read_codes(down, right):
    row, col, level = frame_places()
    col = col + right
    with_rows = ROW * (row + down + WLAT) + LEV * col + level
    with_cols = LON_CODE + (row * 36 + col + WLON) * LEV + level
    return jnp.where((col >= 0) & (col < WLON), with_rows, with_cols)


def one_hot(left, right):
    return jnp.where(left == right, 1.0, 0.0).astype(BF16)


def dot(a, b, dims=(((1,), (0,)), ((), ()))):
    return lax.dot_general(a, b, dims, preferred_element_type=F32)


def kernel(
    sizes, halo, mid, out,
    states, final_cot, step_cot, w_qkv, w_out, land_vec, land_sea, ground, shifts, codes,
    result,
    raw, w_qkv_v, w_out_v, land_vec_v, tables_v, shifts_v, codes_v,
    ext_halo, ext_mid, ext_out, send_cols, pick_halo, pick_cols,
    normed_f, proj, att, cot_f, d_proj, d_mixed, direct,
    local_sem, send_sem, recv_sem, go_sem,
):
    n_lat, n_lon = sizes
    features = raw.shape[-1]
    step, lat, lon = lax.axis_index("step"), lax.axis_index("lat"), lax.axis_index("lon")
    late = step == 1
    early = step == 0

    def around(dy, dx, other=False):
        return (
            1 - step if other else step,
            lax.rem(lat + (dy + n_lat), n_lat),
            lax.rem(lon + (dx + n_lon), n_lon),
        )

    barrier = pltpu.get_barrier_semaphore()
    partners = [(1, 0), (-1, 0), (0, 1), (0, -1), (0, 0, True), (1, 0, True), (-1, 0, True)]
    for partner in partners:
        pl.semaphore_signal(barrier, inc=1, device_id=around(*partner), device_id_type=MESH)

    local = [
        pltpu.make_async_copy(src, dst, local_sem.at[i])
        for i, (src, dst) in enumerate((
            (states, raw.at[0]),
            (step_cot, raw.at[2]),
            (shifts, shifts_v),
            (codes, codes_v),
            (land_sea, tables_v.at[0]),
            (ground, tables_v.at[1]),
            (land_vec, land_vec_v),
            (w_qkv, w_qkv_v),
            (w_out, w_out_v),
        ))
    ]
    (c_state, c_step, c_shift, c_codes, c_land, c_ground, c_vec, c_qkv, c_out) = local
    c_final = pltpu.make_async_copy(final_cot, raw.at[1], local_sem.at[len(local)])
    for copy in local:
        copy.start()

    @pl.when(late)
    def _():
        c_final.start()

    def remote(slot, src, dst, to):
        return pltpu.make_async_remote_copy(
            src_ref=src, dst_ref=dst, send_sem=send_sem.at[slot], recv_sem=recv_sem.at[slot],
            device_id=around(*to), device_id_type=MESH,
        )

    def row_sends(which, exchange, held, other=False, target=None):
        target = held if target is None else target
        return [
            remote(
                4 * which, held.at[pl.ds(exchange.tail, exchange.from_before)],
                target.at[pl.ds(TOK, exchange.from_before)], (1, 0, other),
            ),
            remote(
                4 * which + 1, held.at[pl.ds(0, exchange.from_after)],
                target.at[pl.ds(TOK + exchange.from_before, exchange.from_after)], (-1, 0, other),
            ),
        ]

    def col_sends(which, exchange, held):
        packed = send_cols.at[which]
        return [
            remote(
                4 * which + 2, packed.at[pl.ds(0, exchange.cols_last)],
                held.at[pl.ds(exchange.rows_held, exchange.cols_last)], (0, 1),
            ),
            remote(
                4 * which + 3, packed.at[pl.ds(exchange.cols_last, exchange.cols_first)],
                held.at[pl.ds(exchange.rows_held + exchange.cols_last, exchange.cols_first)], (0, -1),
            ),
        ]

    def started(copies):
        for copy in copies:
            copy.start()

    def arrived(copies):
        for copy in copies:
            copy.wait_recv()

    halo_rows = [row_sends(i, halo, ext_halo.at[i]) for i in range(2)]
    halo_cols = [col_sends(i, halo, ext_halo.at[i]) for i in range(2)]
    mid_rows = row_sends(2, mid, ext_out, True, ext_mid)
    mid_rows.append(remote(16, ext_out.at[pl.ds(0, TOK)], ext_mid.at[pl.ds(0, TOK)], (0, 0, True)))
    mid_cols = col_sends(2, mid, ext_mid)
    out_rows = row_sends(3, out, ext_out)
    out_cols = col_sends(3, out, ext_out)

    def forward_cols(which, exchange, held, picked):
        rows = dot(picked, held[pl.ds(0, exchange.rows_held)])
        send_cols[which, pl.ds(0, exchange.cols_sent)] = rows.astype(BF16)

    c_state.wait()
    ext_halo[0, pl.ds(0, TOK)] = raw[0].reshape(TOK, features)
    pl.semaphore_wait(barrier, len(partners))

    @pl.when(late)
    def _():
        started(halo_rows[0])

    c_step.wait()

    @pl.when(late)
    def _():
        c_final.wait()
        ext_halo[1, pl.ds(0, TOK)] = raw[1].reshape(TOK, features)
        direct[...] = raw[2].reshape(TOK, features)

    @pl.when(early)
    def _():
        ext_halo[1, pl.ds(0, TOK)] = raw[2].reshape(TOK, features)
        direct[...] = jnp.zeros((TOK, features), BF16)

    c_shift.wait()

    def start_of(row):
        a, b = shifts_v[row, 0], shifts_v[row, 1]
        return jnp.where(a >= 3, a - WLAT, a), jnp.where(b >= 6, b - WLON, b)

    s_late, t_late = start_of(1)
    s_early, t_early = start_of(0)
    s = jnp.where(late, s_late, s_early)
    t = jnp.where(late, t_late, t_early)
    c_codes.wait()
    pick_cols[...] = one_hot(halo.sent_codes(s), codes_v[0:1, : halo.rows_held])
    pick_halo[...] = one_hot(read_codes(s, t), codes_v[0:1, : halo.held])

    row, col, level = frame_places()
    lat_total, lon_total = tables_v.shape[1], tables_v.shape[2]
    at_row = lat * WLAT + s + row
    at_row = jnp.where(at_row < 0, at_row + lat_total, jnp.where(at_row >= lat_total, at_row - lat_total, at_row))
    at_col = lon * WLON + t + col
    at_col = jnp.where(at_col < 0, at_col + lon_total, jnp.where(at_col >= lon_total, at_col - lon_total, at_col))
    c_land.wait()
    c_ground.wait()
    row_pick = one_hot(at_row, lax.broadcasted_iota(jnp.int32, (TOK, lat_total), 1))
    col_pick = at_col == lax.broadcasted_iota(jnp.int32, (TOK, lon_total), 1)

    def looked_up(i):
        lines = dot(row_pick, tables_v[i].astype(F32).astype(BF16))
        return jnp.sum(jnp.where(col_pick, lines, 0.0), axis=1, keepdims=True)

    land = looked_up(0)
    key_valid = jnp.where(level.astype(F32) >= looked_up(1), 1.0, 0.0)
    shift_lat = jnp.where(s < 0, s + WLAT, s)
    window = jnp.where(s < 0, lax.rem(lat + (n_lat - 1), n_lat), lat)
    first_seam = jnp.where(window == n_lat - 1, WLAT - shift_lat, WLAT)
    lane = lax.broadcasted_iota(jnp.int32, (1, 2 * TOK), 1)
    lane = jnp.where(lane >= TOK, lane - TOK, lane)
    seam_key = jnp.where(row >= first_seam, 1, 0)
    seam_query = jnp.where(quotient(lane >> 1, WLON) >= first_seam, 1, 0)
    allowed = jnp.where(seam_key == seam_query, key_valid, 0.0)
    c_vec.wait()

    @pl.when(early)
    def _():
        pl.semaphore_wait(go_sem, 1)
        started(halo_rows[0] + halo_rows[1])

    arrived(halo_rows[0])

    @pl.when(late)
    def _():
        started(halo_rows[1])

    forward_cols(0, halo, ext_halo.at[0], pick_cols[...])
    started(halo_cols[0])
    arrived(halo_cols[0])

    lifted = dot(pick_halo[...], ext_halo[0]) + land * land_vec_v[...]
    centred = lifted - jnp.mean(lifted, axis=1, keepdims=True)
    scale = lax.rsqrt(jnp.mean(centred * centred, axis=1, keepdims=True) + 1e-05)
    normed = centred * scale
    normed_f[...] = normed
    c_qkv.wait()
    proj[...] = dot(normed.astype(BF16), w_qkv_v[...]).astype(BF16)

    arrived(halo_rows[1])

    @pl.when(late)
    def _():
        pl.semaphore_signal(go_sem, inc=1, device_id=around(0, 0, True), device_id_type=MESH)

    forward_cols(1, halo, ext_halo.at[1], pick_cols[...])
    started(halo_cols[1])

    half = lax.broadcasted_iota(jnp.int32, (TOK, 128), 1) < 64
    zero = jnp.zeros((TOK, 128), BF16)

    def both_heads(pair):
        return jnp.concatenate([jnp.where(half, pair, zero), jnp.where(half, zero, pair)], axis=0)

    def queries(p):
        return both_heads(proj[:, p * 128 : (p + 1) * 128] * 0.125)

    def keys(p):
        return proj[:, features + p * 128 : features + (p + 1) * 128]

    def values(p):
        return proj[:, 2 * features + p * 128 : 2 * features + (p + 1) * 128]

    for p in range(HEADS // 2):
        weights = jnp.exp(dot(keys(p), queries(p), NT)) * allowed
        att[p] = weights * (1.0 / jnp.sum(weights, axis=0, keepdims=True))

    arrived(halo_cols[1])
    cot_f[...] = dot(pick_halo[...], ext_halo[1])

    @pl.when(early)
    def _():
        down, right = s_early - s_late, t_early - t_late
        picked = one_hot(mid.sent_codes(down), codes_v[1:2, : mid.rows_held])
        pick = one_hot(read_codes(down, right), codes_v[1:2, : mid.held])
        arrived(mid_rows)
        pl.semaphore_signal(go_sem, inc=1, device_id=around(0, 0, True), device_id_type=MESH)
        forward_cols(2, mid, ext_mid, picked)
        started(mid_cols)
        arrived(mid_cols)
        cot_f[...] += dot(pick, ext_mid[...])

    cot_w = cot_f[...].astype(BF16)

    c_out.wait()
    d_mixed[...] = dot(cot_w, w_out_v[...], NT).astype(BF16)
    for p in range(HEADS // 2):
        d_both = both_heads(d_mixed[:, p * 128 : (p + 1) * 128])
        query, key, attention = queries(p), keys(p), att[p]
        inner = attention * dot(values(p), d_both, NT)
        d_scores = (inner - attention * jnp.sum(inner, axis=0, keepdims=True)).astype(BF16)
        d_query = dot(d_scores, key, TN)
        d_query = jnp.where(half, d_query[:TOK], d_query[TOK:]) * 0.125
        d_proj[:, p * 128 : (p + 1) * 128] = d_query.astype(BF16)
        d_proj[:, features + p * 128 : features + (p + 1) * 128] = dot(d_scores, query).astype(BF16)
        d_proj[:, 2 * features + p * 128 : 2 * features + (p + 1) * 128] = dot(attention.astype(BF16), d_both).astype(BF16)
    d_normed = dot(d_proj[...], w_qkv_v[...], NT).astype(BF16).astype(F32)
    normed = normed_f[...]
    along = jnp.mean(d_normed * normed, axis=1, keepdims=True)
    total = cot_w.astype(F32) + scale * (d_normed - jnp.mean(d_normed, axis=1, keepdims=True) - normed * along)
    ext_out[pl.ds(0, TOK)] = total.astype(BF16)

    @pl.when(late)
    def _():
        started(mid_rows)
        pl.semaphore_wait(go_sem, 1)

    started(out_rows)
    picked = one_hot(out.sent_codes(-s), codes_v[2:3, : out.rows_held])
    pick_out = one_hot(read_codes(-s, -t), codes_v[2:3, : out.held])
    arrived(out_rows)
    forward_cols(3, out, ext_out, picked)
    started(out_cols)
    arrived(out_cols)
    home = dot(pick_out, ext_out[...]) + direct[...].astype(F32)
    result[...] = home.astype(BF16).reshape(result.shape)

    for copy in halo_rows[0] + halo_cols[0] + halo_rows[1] + halo_cols[1] + out_rows + out_cols:
        copy.wait_send()

    @pl.when(late)
    def _():
        for copy in mid_rows:
            copy.wait_send()

    @pl.when(early)
    def _():
        for copy in mid_cols:
            copy.wait_send()


def per_device(sizes, states, final_cot, step_cot, w_qkv, w_out, land_vec, land_sea, ground, shifts):
    halo = Exchange(2, 3, 5, 6)
    mid = Exchange(3, 3, 6, 6)
    out = Exchange(3, 2, 6, 5)
    features = w_qkv.shape[0]
    codes = np.full((8, 512), -1, np.int32)
    for i, e in enumerate((halo, mid, out)):
        codes[i, : e.held] = e.codes
    held_spec = pl.BlockSpec(memory_space=pltpu.HBM)

    def field(*shape):
        return pltpu.VMEM(shape, BF16)

    def home(block):
        return jnp.moveaxis(block, 0, 2).reshape(TOK // LEV, LEV, features)

    gradient = pl.pallas_call(
        functools.partial(kernel, sizes, halo, mid, out),
        out_shape=jax.ShapeDtypeStruct((TOK // LEV, LEV, features), BF16),
        in_specs=[held_spec] * 10,
        out_specs=pl.BlockSpec(memory_space=pltpu.VMEM),
        scratch_shapes=[
            field(3, TOK // LEV, LEV, features),
            field(*w_qkv.shape),
            field(*w_out.shape),
            pltpu.VMEM((1, features), F32),
            pltpu.VMEM((2,) + land_sea.shape, jnp.int32),
            pltpu.SMEM(shifts.shape, jnp.int32),
            pltpu.VMEM(codes.shape, jnp.int32),
            field(2, halo.held, features),
            field(mid.held, features),
            field(out.held, features),
            field(4, max(e.cols_sent for e in (halo, mid, out)), features),
            field(TOK, halo.held),
            field(halo.cols_sent, halo.rows_held),
            pltpu.VMEM((TOK, features), F32),
            field(TOK, 3 * features),
            pltpu.VMEM((HEADS // 2, TOK, 2 * TOK), F32),
            pltpu.VMEM((TOK, features), F32),
            field(TOK, 3 * features),
            field(TOK, features),
            field(TOK, features),
            pltpu.SemaphoreType.DMA((10,)),
            pltpu.SemaphoreType.DMA((17,)),
            pltpu.SemaphoreType.DMA((17,)),
            pltpu.SemaphoreType.REGULAR,
        ],
        compiler_params=pltpu.CompilerParams(
            collective_id=0, has_side_effects=True, vmem_limit_bytes=60 * 1024 * 1024
        ),
    )(
        home(states[0]), home(final_cot), home(step_cot), w_qkv, w_out, land_vec.reshape(1, features),
        land_sea, ground, shifts, jnp.asarray(codes),
    )
    return jnp.moveaxis(gradient.reshape(WLAT, WLON, LEV, features), 2, 0)[None]


def solution(mesh):
    return jax.shard_map(
        functools.partial(per_device, (mesh.shape["lat"], mesh.shape["lon"])),
        mesh=mesh,
        in_specs=(
            P("step", None, "lat", "lon", None),
            P(None, "lat", "lon", None),
            P(None, "lat", "lon", None),
            P(),
            P(),
            P(),
            P(),
            P(),
            P(),
        ),
        out_specs=P("step", None, "lat", "lon", None),
        check_vma=False,
    )
```

```python
import functools

import jax
import jax.numpy as jnp
import numpy as np
from jax import lax
from jax.experimental import pallas as pl
from jax.experimental.pallas import tpu as pltpu
from jax.sharding import PartitionSpec as P

HEADS = 8
LEV = 2
WLAT = 6
WLON = 12
ROW = WLON * LEV
TOK = WLAT * ROW
MESH = pl.DeviceIdType.MESH
F32 = jnp.float32
BF16 = jnp.bfloat16
NT = (((1,), (1,)), ((), ()))
TN = (((0,), (0,)), ((), ()))


def up_to(value, unit):
    return -(-value // unit) * unit


class Exchange:
    def __init__(self, first_rows, last_rows, first_cols, last_cols):
        rows = {-1: range(first_rows), 0: range(WLAT), 1: range(WLAT - last_rows, WLAT)}
        cols = {-1: range(first_cols), 0: range(WLON), 1: range(WLON - last_cols, WLON)}
        self.pieces = []
        packed, codes = [], list(range(4 * TOK, 5 * TOK))
        offset = 0
        for dy, dx in ((1, 1), (1, -1), (-1, 1), (-1, -1), (1, 0), (-1, 0), (0, 1), (0, -1)):
            tokens = [(r * WLON + c) * LEV + l for r in rows[dy] for c in cols[dx] for l in range(LEV)]
            if not tokens:
                continue
            size = up_to(len(tokens), 16)
            zone = (1 - dy) * 3 + 1 - dx
            filler = [-1] * (size - len(tokens))
            codes += [zone * TOK + token for token in tokens] + filler
            packed += tokens + filler
            self.pieces.append((dy, dx, offset, size))
            offset += size
        self.sent = offset
        self.held = TOK + offset
        self.codes, self.packed = np.array(codes, np.int32), np.array(packed, np.int32)


def quotient(value, by):
    factor = (1 << 14) // by + 1
    assert all((i * factor) >> 14 == i // by for i in range(TOK + 1))
    return (value * factor) >> 14


def frame_places():
    index = lax.broadcasted_iota(jnp.int32, (TOK, 1), 0)
    place = index >> 1
    row = quotient(place, WLON)
    return row, place - row * WLON, index & 1


def read_codes(down, right):
    row, col, level = frame_places()
    row, col = row + down, col + right
    zone_row = jnp.where(row >= WLAT, 1, 0) - jnp.where(row < 0, 1, 0)
    zone_col = jnp.where(col >= WLON, 1, 0) - jnp.where(col < 0, 1, 0)
    place = (row - zone_row * WLAT) * WLON + col - zone_col * WLON
    return ((zone_row + 1) * 3 + zone_col + 1) * TOK + place * LEV + level


def one_hot(left, right):
    return jnp.where(left == right, 1.0, 0.0).astype(BF16)


def dot(a, b, dims=(((1,), (0,)), ((), ()))):
    return lax.dot_general(a, b, dims, preferred_element_type=F32)


def kernel(
    sizes, starts, halo, mid, out,
    states, final_cot, step_cot, w_qkv, w_out, land_vec, land_sea, ground, shifts, codes,
    result,
    raw, w_qkv_v, w_out_v, land_vec_v, tables_v, shifts_v, codes_v,
    ext_halo, ext_mid, ext_out, send_halo, send_mid, send_out,
    normed_f, proj, att, cot_f, d_proj, d_mixed, direct,
    local_sem, send_sem, recv_sem,
):
    n_lat, n_lon = sizes
    features = w_qkv.shape[0]
    pairs = HEADS // 2
    step, lat, lon = lax.axis_index("step"), lax.axis_index("lat"), lax.axis_index("lon")
    late = step == 1
    early = step == 0

    def around(dy, dx, other=False):
        return (
            1 - step if other else step,
            lax.rem(lat + (dy + n_lat), n_lat),
            lax.rem(lon + (dx + n_lon), n_lon),
        )

    to_early = [(0, 0)] + [(dy, dx) for dy, dx, _, _ in mid.pieces]
    to_same = sorted(
        {(dy, dx) for dy, dx, _, _ in halo.pieces + out.pieces} | {(-dy, -dx) for dy, dx, _, _ in halo.pieces + out.pieces}
    )
    sign = 2 * step - 1
    barrier = pltpu.get_barrier_semaphore()
    for dy, dx in to_same:
        pl.semaphore_signal(barrier, inc=1, device_id=around(dy, dx), device_id_type=MESH)
    for dy, dx in to_early:
        pl.semaphore_signal(barrier, inc=1, device_id=around(dy * sign, dx * sign, True), device_id_type=MESH)

    local = [
        pltpu.make_async_copy(src, dst, local_sem.at[i])
        for i, (src, dst) in enumerate((
            (states, raw.at[0]),
            (codes, codes_v),
            (step_cot, raw.at[2]),
            (shifts, shifts_v),
            (land_sea, tables_v.at[0]),
            (ground, tables_v.at[1]),
            (land_vec, land_vec_v),
            (w_qkv, w_qkv_v),
            (w_out, w_out_v),
            (final_cot, raw.at[1]),
        ))
    ]
    (c_state, c_codes, c_step, c_shift, c_land, c_ground, c_vec, c_qkv, c_out, c_final) = local
    for copy in local:
        copy.start()

    def remotes(first, exchange, src, dst, other=False):
        return [
            pltpu.make_async_remote_copy(
                src_ref=src.at[pl.ds(offset, size)], dst_ref=dst.at[pl.ds(TOK + offset, size)],
                send_sem=send_sem.at[first + k], recv_sem=recv_sem.at[first + k],
                device_id=around(dy, dx, other), device_id_type=MESH,
            )
            for k, (dy, dx, offset, size) in enumerate(exchange.pieces)
        ]

    halo_sends = [remotes(8 * i, halo, send_halo.at[i], ext_halo.at[i]) for i in range(2)]
    out_sends = remotes(16, out, send_out, ext_out)
    mid_sends = [pltpu.make_async_remote_copy(
        src_ref=ext_out.at[pl.ds(0, TOK)], dst_ref=ext_mid.at[pl.ds(0, TOK)],
        send_sem=send_sem.at[32], recv_sem=recv_sem.at[32], device_id=around(0, 0, True), device_id_type=MESH,
    )] + remotes(24, mid, send_mid, ext_mid, True)

    def started(copies):
        for copy in copies:
            copy.start()

    def arrived(copies):
        for copy in copies:
            copy.wait_recv()

    def packing(row, exchange):
        token = lax.broadcasted_iota(jnp.int32, (TOK, exchange.sent), 0)
        return one_hot(token, codes_v[row : row + 1, : exchange.sent])

    c_codes.wait()
    pack_halo = packing(3, halo)
    c_state.wait()
    c_step.wait()
    c_final.wait()
    ext_halo[0, pl.ds(0, TOK)] = raw[0].reshape(TOK, features)
    send_halo[0] = dot(pack_halo, ext_halo[0, pl.ds(0, TOK)], TN).astype(BF16)
    pl.semaphore_wait(barrier, len(to_same) + len(to_early))
    started(halo_sends[0])
    ext_halo[1, pl.ds(0, TOK)] = raw[2 - step].reshape(TOK, features)
    send_halo[1] = dot(pack_halo, ext_halo[1, pl.ds(0, TOK)], TN).astype(BF16)
    started(halo_sends[1])

    @pl.when(late)
    def _():
        direct[...] = raw[2].reshape(TOK, features)

    @pl.when(early)
    def _():
        direct[...] = jnp.zeros((TOK, features), BF16)

    c_shift.wait()
    s_early, s_late = starts
    t_early, t_late = (jnp.where(b >= 6, b - WLON, b) for b in (shifts_v[0, 1], shifts_v[1, 1]))
    s = jnp.where(late, s_late, s_early)
    t = jnp.where(late, t_late, t_early)
    pick_halo = one_hot(read_codes(s, t), codes_v[0:1, : halo.held])

    row, col, level = frame_places()
    lat_total, lon_total = tables_v.shape[1], tables_v.shape[2]
    at_row = lat * WLAT + s + row
    at_row = jnp.where(at_row < 0, at_row + lat_total, jnp.where(at_row >= lat_total, at_row - lat_total, at_row))
    at_col = lon * WLON + t + col
    at_col = jnp.where(at_col < 0, at_col + lon_total, jnp.where(at_col >= lon_total, at_col - lon_total, at_col))
    c_land.wait()
    c_ground.wait()
    row_pick = one_hot(at_row, lax.broadcasted_iota(jnp.int32, (TOK, lat_total), 1))
    col_pick = at_col == lax.broadcasted_iota(jnp.int32, (TOK, lon_total), 1)

    def looked_up(table):
        lines = dot(row_pick, table.astype(F32).astype(BF16))
        return jnp.sum(jnp.where(col_pick, lines, 0.0), axis=1, keepdims=True)

    both = looked_up(tables_v[0] + 2 * tables_v[1])
    ground_at = jnp.where(both >= 1.5, 1.0, 0.0)
    land = both - 2.0 * ground_at
    key_valid = jnp.where(level.astype(F32) >= ground_at, 1.0, 0.0)
    shift_lat = jnp.where(s < 0, s + WLAT, s)
    window = jnp.where(s < 0, lax.rem(lat + (n_lat - 1), n_lat), lat)
    first_seam = jnp.where(window == n_lat - 1, WLAT - shift_lat, WLAT)
    lane = lax.broadcasted_iota(jnp.int32, (1, 2 * TOK), 1)
    lane = jnp.where(lane >= TOK, lane - TOK, lane)
    seam_key = jnp.where(row >= first_seam, 1, 0)
    seam_query = jnp.where(quotient(lane >> 1, WLON) >= first_seam, 1, 0)
    allowed = jnp.where(seam_key == seam_query, key_valid, 0.0)
    c_vec.wait()
    c_qkv.wait()
    arrived(halo_sends[0])

    lifted = dot(pick_halo, ext_halo[0]) + land * land_vec_v[...]
    centred = lifted - jnp.mean(lifted, axis=1, keepdims=True)
    scale = lax.rsqrt(jnp.mean(centred * centred, axis=1, keepdims=True) + 1e-05)
    normed = centred * scale
    normed_f[...] = normed
    projected = dot(normed.astype(BF16), w_qkv_v[...]).astype(BF16)
    for p in range(3 * pairs):
        proj[p] = projected[:, p * 128 : (p + 1) * 128]
    half = lax.broadcasted_iota(jnp.int32, (TOK, 128), 1) < 64
    zero = jnp.zeros((TOK, 128), BF16)

    def both_heads(pair):
        return jnp.concatenate([jnp.where(half, pair, zero), jnp.where(half, zero, pair)], axis=0)

    @pl.loop(0, pairs)
    def _(p):
        weights = jnp.exp(dot(proj[pairs + p], both_heads(proj[p] * 0.125), NT)) * allowed
        att[p] = weights * (1.0 / jnp.sum(weights, axis=0, keepdims=True))

    arrived(halo_sends[1])
    cot_f[...] = dot(pick_halo, ext_halo[1])
    c_out.wait()

    @pl.when(early)
    def _():
        pick = one_hot(read_codes(s_early - s_late, t_early - t_late), codes_v[1:2, : mid.held])
        arrived(mid_sends)
        cot_f[...] += dot(pick, ext_mid[...])

    cot_w = cot_f[...].astype(BF16)

    d_all = dot(cot_w, w_out_v[...], NT).astype(BF16)
    for p in range(pairs):
        d_mixed[p] = d_all[:, p * 128 : (p + 1) * 128]

    @pl.loop(0, pairs)
    def _(p):
        d_both = both_heads(d_mixed[p])
        attention = att[p]
        inner = attention * dot(proj[2 * pairs + p], d_both, NT)
        d_scores = (inner - attention * jnp.sum(inner, axis=0, keepdims=True)).astype(BF16)
        d_query = dot(d_scores, proj[pairs + p], TN)
        d_query = jnp.where(half, d_query[:TOK], d_query[TOK:]) * 0.125
        d_proj[p] = d_query.astype(BF16)
        d_proj[pairs + p] = dot(d_scores, both_heads(proj[p] * 0.125)).astype(BF16)
        d_proj[2 * pairs + p] = dot(attention.astype(BF16), d_both).astype(BF16)

    d_all = jnp.concatenate([d_proj[p] for p in range(3 * pairs)], axis=1)
    d_normed = dot(d_all, w_qkv_v[...], NT).astype(BF16).astype(F32)
    normed = normed_f[...]
    along = jnp.mean(d_normed * normed, axis=1, keepdims=True)
    total = cot_w.astype(F32) + scale * (d_normed - jnp.mean(d_normed, axis=1, keepdims=True) - normed * along)
    ext_out[pl.ds(0, TOK)] = total.astype(BF16)

    @pl.when(late)
    def _():
        mid_sends[0].start()
        send_mid[...] = dot(packing(4, mid), ext_out[pl.ds(0, TOK)], TN).astype(BF16)
        started(mid_sends[1:])

    send_out[...] = dot(packing(5, out), ext_out[pl.ds(0, TOK)], TN).astype(BF16)
    started(out_sends)
    pick_out = one_hot(read_codes(-s, -t), codes_v[2:3, : out.held])
    arrived(out_sends)
    home = dot(pick_out, ext_out[...]) + direct[...].astype(F32)
    result[...] = home.astype(BF16).reshape(result.shape)

    for copy in halo_sends[0] + halo_sends[1] + out_sends:
        copy.wait_send()

    @pl.when(late)
    def _():
        for copy in mid_sends:
            copy.wait_send()


def variant(sizes, number, starts, states, final_cot, step_cot, w_qkv, w_out, land_vec, land_sea, ground, shifts):
    before, after = max(-min(starts), 0), max(max(starts), 0)
    apart = starts[0] - starts[1]
    halo = Exchange(after, before, 5, 6)
    mid = Exchange(max(apart, 0), max(-apart, 0), 6, 6)
    out = Exchange(before, after, 6, 5)
    features = w_qkv.shape[0]
    codes = np.full((8, 512), -1, np.int32)
    for i, e in enumerate((halo, mid, out)):
        codes[i, : e.held] = e.codes
        codes[3 + i, : e.sent] = e.packed
    held_spec = pl.BlockSpec(memory_space=pltpu.HBM)

    def field(*shape):
        return pltpu.VMEM(shape, BF16)

    def home(block):
        return jnp.moveaxis(block, 0, 2).reshape(TOK // LEV, LEV, features)

    gradient = pl.pallas_call(
        functools.partial(kernel, sizes, starts, halo, mid, out),
        out_shape=jax.ShapeDtypeStruct((TOK // LEV, LEV, features), BF16),
        in_specs=[held_spec] * 10,
        out_specs=pl.BlockSpec(memory_space=pltpu.VMEM),
        scratch_shapes=[
            field(3, TOK // LEV, LEV, features),
            field(*w_qkv.shape),
            field(*w_out.shape),
            pltpu.VMEM((1, features), F32),
            pltpu.VMEM((2,) + land_sea.shape, jnp.int32),
            pltpu.SMEM(shifts.shape, jnp.int32),
            pltpu.VMEM(codes.shape, jnp.int32),
            field(2, halo.held, features),
            field(mid.held, features),
            field(out.held, features),
            field(2, halo.sent, features),
            field(mid.sent, features),
            field(out.sent, features),
            pltpu.VMEM((TOK, features), F32),
            field(3 * HEADS // 2, TOK, 128),
            pltpu.VMEM((HEADS // 2, TOK, 2 * TOK), F32),
            pltpu.VMEM((TOK, features), F32),
            field(3 * HEADS // 2, TOK, 128),
            field(HEADS // 2, TOK, 128),
            field(TOK, features),
            pltpu.SemaphoreType.DMA((10,)),
            pltpu.SemaphoreType.DMA((33,)),
            pltpu.SemaphoreType.DMA((33,)),
        ],
        compiler_params=pltpu.CompilerParams(
            collective_id=number, has_side_effects=True, vmem_limit_bytes=60 * 1024 * 1024
        ),
    )(
        home(states[0]), home(final_cot), home(step_cot), w_qkv, w_out, land_vec.reshape(1, features),
        land_sea, ground, shifts, jnp.asarray(codes),
    )
    return jnp.moveaxis(gradient.reshape(WLAT, WLON, LEV, features), 2, 0)[None]


def per_device(sizes, *operands):
    others = (1, 2, 3 - WLAT, 4 - WLAT, -1)
    pairs = [(start, -1) for start in others] + [(-1, start) for start in others[:-1]]
    shifts = operands[-1]
    case = jnp.where(shifts[1, 0] == 5, shifts[0, 0] - 1, shifts[1, 0] + 4)
    cases = [functools.partial(variant, sizes, number, pair) for number, pair in enumerate(pairs)]
    return lax.switch(case, cases, *operands)


def solution(mesh):
    return jax.shard_map(
        functools.partial(per_device, (mesh.shape["lat"], mesh.shape["lon"])),
        mesh=mesh,
        in_specs=(
            P("step", None, "lat", "lon", None),
            P(None, "lat", "lon", None),
            P(None, "lat", "lon", None),
            P(),
            P(),
            P(),
            P(),
            P(),
            P(),
        ),
        out_specs=P("step", None, "lat", "lon", None),
        check_vma=False,
    )
```

```python
import functools

import jax
import jax.numpy as jnp
import numpy as np
from jax import lax
from jax.experimental import pallas as pl
from jax.experimental.pallas import tpu as pltpu
from jax.sharding import PartitionSpec as P

HEADS = 8
LEV = 2
WLAT = 6
WLON = 12
ROW = WLON * LEV
TOK = WLAT * ROW
MESH = pl.DeviceIdType.MESH
F32 = jnp.float32
BF16 = jnp.bfloat16
NT = (((1,), (1,)), ((), ()))
TN = (((0,), (0,)), ((), ()))


def up_to(value, unit):
    return -(-value // unit) * unit


class Exchange:
    def __init__(self, first_rows, last_rows, first_cols, last_cols):
        rows = {-1: range(first_rows), 0: range(WLAT), 1: range(WLAT - last_rows, WLAT)}
        cols = {-1: range(first_cols), 0: range(WLON), 1: range(WLON - last_cols, WLON)}
        self.pieces = []
        packed, codes = [], list(range(4 * TOK, 5 * TOK))
        offset = 0
        for dy, dx in ((1, 1), (1, -1), (-1, 1), (-1, -1), (1, 0), (-1, 0), (0, 1), (0, -1)):
            tokens = [(r * WLON + c) * LEV + l for r in rows[dy] for c in cols[dx] for l in range(LEV)]
            if not tokens:
                continue
            size = up_to(len(tokens), 16)
            zone = (1 - dy) * 3 + 1 - dx
            filler = [-1] * (size - len(tokens))
            codes += [zone * TOK + token for token in tokens] + filler
            packed += tokens + filler
            self.pieces.append((dy, dx, offset, size))
            offset += size
        self.sent = offset
        self.held = TOK + offset
        self.codes, self.packed = np.array(codes, np.int32), np.array(packed, np.int32)


def quotient(value, by):
    factor = (1 << 14) // by + 1
    assert all((i * factor) >> 14 == i // by for i in range(TOK + 1))
    return (value * factor) >> 14


def frame_places():
    index = lax.broadcasted_iota(jnp.int32, (TOK, 1), 0)
    place = index >> 1
    row = quotient(place, WLON)
    return row, place - row * WLON, index & 1


def read_codes(down, right):
    row, col, level = frame_places()
    row, col = row + down, col + right
    zone_row = jnp.where(row >= WLAT, 1, 0) - jnp.where(row < 0, 1, 0)
    zone_col = jnp.where(col >= WLON, 1, 0) - jnp.where(col < 0, 1, 0)
    place = (row - zone_row * WLAT) * WLON + col - zone_col * WLON
    return ((zone_row + 1) * 3 + zone_col + 1) * TOK + place * LEV + level


def one_hot(left, right):
    return jnp.where(left == right, 1.0, 0.0).astype(BF16)


def dot(a, b, dims=(((1,), (0,)), ((), ()))):
    return lax.dot_general(a, b, dims, preferred_element_type=F32)


def kernel(
    sizes, starts, halo, mid, out,
    states, final_cot, step_cot, w_qkv, w_out, land_vec, land_sea, ground, shifts, codes,
    result,
    raw, w_qkv_v, w_out_v, land_vec_v, tables_v, shifts_v, codes_v,
    ext_halo, ext_mid, ext_out, send_halo, send_mid, send_out,
    normed_f, proj, att, cot_f, d_proj, d_mixed, direct,
    local_sem, send_sem, recv_sem, go_sem,
):
    n_lat, n_lon = sizes
    features = w_qkv.shape[0]
    pairs = HEADS // 2
    step, lat, lon = lax.axis_index("step"), lax.axis_index("lat"), lax.axis_index("lon")
    late = step == 1
    early = step == 0

    def around(dy, dx, other=False):
        return (
            1 - step if other else step,
            lax.rem(lat + (dy + n_lat), n_lat),
            lax.rem(lon + (dx + n_lon), n_lon),
        )

    to_early = [(0, 0)] + [(dy, dx) for dy, dx, _, _ in mid.pieces]
    to_same = sorted(
        {(dy, dx) for dy, dx, _, _ in halo.pieces + out.pieces} | {(-dy, -dx) for dy, dx, _, _ in halo.pieces + out.pieces}
    )
    sign = 2 * step - 1
    barrier = pltpu.get_barrier_semaphore()
    for dy, dx in to_same:
        pl.semaphore_signal(barrier, inc=1, device_id=around(dy, dx), device_id_type=MESH)
    for dy, dx in to_early:
        pl.semaphore_signal(barrier, inc=1, device_id=around(dy * sign, dx * sign, True), device_id_type=MESH)

    local = [
        pltpu.make_async_copy(src, dst, local_sem.at[i])
        for i, (src, dst) in enumerate((
            (states, raw.at[0]),
            (codes, codes_v),
            (step_cot, raw.at[2]),
            (shifts, shifts_v),
            (land_sea, tables_v.at[0]),
            (ground, tables_v.at[1]),
            (land_vec, land_vec_v),
            (w_qkv, w_qkv_v),
            (w_out, w_out_v),
            (final_cot, raw.at[1]),
        ))
    ]
    (c_state, c_codes, c_step, c_shift, c_land, c_ground, c_vec, c_qkv, c_out, c_final) = local
    for copy in local:
        copy.start()

    def remotes(first, exchange, src, dst, other=False):
        return [
            pltpu.make_async_remote_copy(
                src_ref=src.at[pl.ds(offset, size)], dst_ref=dst.at[pl.ds(TOK + offset, size)],
                send_sem=send_sem.at[first + k], recv_sem=recv_sem.at[first + k],
                device_id=around(dy, dx, other), device_id_type=MESH,
            )
            for k, (dy, dx, offset, size) in enumerate(exchange.pieces)
        ]

    halo_sends = [remotes(8 * i, halo, send_halo.at[i], ext_halo.at[i]) for i in range(2)]
    out_sends = remotes(16, out, send_out, ext_out)
    mid_sends = [pltpu.make_async_remote_copy(
        src_ref=ext_out.at[pl.ds(0, TOK)], dst_ref=ext_mid.at[pl.ds(0, TOK)],
        send_sem=send_sem.at[32], recv_sem=recv_sem.at[32], device_id=around(0, 0, True), device_id_type=MESH,
    )] + remotes(24, mid, send_mid, ext_mid, True)

    def started(copies):
        for copy in copies:
            copy.start()

    def arrived(copies):
        for copy in copies:
            copy.wait_recv()

    def packing(row, exchange):
        token = lax.broadcasted_iota(jnp.int32, (TOK, exchange.sent), 0)
        return one_hot(token, codes_v[row : row + 1, : exchange.sent])

    c_codes.wait()
    pack_halo = packing(3, halo)
    c_state.wait()
    c_step.wait()
    c_final.wait()
    ext_halo[0, pl.ds(0, TOK)] = raw[0].reshape(TOK, features)
    send_halo[0] = dot(pack_halo, ext_halo[0, pl.ds(0, TOK)], TN).astype(BF16)
    pl.semaphore_wait(barrier, len(to_same) + len(to_early))

    @pl.when(late)
    def _():
        started(halo_sends[0])

    ext_halo[1, pl.ds(0, TOK)] = raw[2 - step].reshape(TOK, features)
    send_halo[1] = dot(pack_halo, ext_halo[1, pl.ds(0, TOK)], TN).astype(BF16)

    @pl.when(late)
    def _():
        direct[...] = raw[2].reshape(TOK, features)

    @pl.when(early)
    def _():
        direct[...] = jnp.zeros((TOK, features), BF16)

    c_shift.wait()
    s_early, s_late = starts
    t_early, t_late = (jnp.where(b >= 6, b - WLON, b) for b in (shifts_v[0, 1], shifts_v[1, 1]))
    s = jnp.where(late, s_late, s_early)
    t = jnp.where(late, t_late, t_early)
    pick_halo = one_hot(read_codes(s, t), codes_v[0:1, : halo.held])

    row, col, level = frame_places()
    lat_total, lon_total = tables_v.shape[1], tables_v.shape[2]
    at_row = lat * WLAT + s + row
    at_row = jnp.where(at_row < 0, at_row + lat_total, jnp.where(at_row >= lat_total, at_row - lat_total, at_row))
    at_col = lon * WLON + t + col
    at_col = jnp.where(at_col < 0, at_col + lon_total, jnp.where(at_col >= lon_total, at_col - lon_total, at_col))
    c_land.wait()
    c_ground.wait()
    row_pick = one_hot(at_row, lax.broadcasted_iota(jnp.int32, (TOK, lat_total), 1))
    col_pick = at_col == lax.broadcasted_iota(jnp.int32, (TOK, lon_total), 1)

    def looked_up(table):
        lines = dot(row_pick, table.astype(F32).astype(BF16))
        return jnp.sum(jnp.where(col_pick, lines, 0.0), axis=1, keepdims=True)

    both = looked_up(tables_v[0] + 2 * tables_v[1])
    ground_at = jnp.where(both >= 1.5, 1.0, 0.0)
    land = both - 2.0 * ground_at
    key_valid = jnp.where(level.astype(F32) >= ground_at, 1.0, 0.0)
    shift_lat = jnp.where(s < 0, s + WLAT, s)
    window = jnp.where(s < 0, lax.rem(lat + (n_lat - 1), n_lat), lat)
    first_seam = jnp.where(window == n_lat - 1, WLAT - shift_lat, WLAT)
    lane = lax.broadcasted_iota(jnp.int32, (1, 2 * TOK), 1)
    lane = jnp.where(lane >= TOK, lane - TOK, lane)
    seam_key = jnp.where(row >= first_seam, 1, 0)
    seam_query = jnp.where(quotient(lane >> 1, WLON) >= first_seam, 1, 0)
    allowed = jnp.where(seam_key == seam_query, key_valid, 0.0)
    c_vec.wait()
    c_qkv.wait()

    @pl.when(late)
    def _():
        started(halo_sends[1])
        arrived(halo_sends[0])
        pl.semaphore_signal(go_sem, inc=1, device_id=around(0, 0, True), device_id_type=MESH)

    @pl.when(early)
    def _():
        pl.semaphore_wait(go_sem, 1)
        started(halo_sends[0] + halo_sends[1])
        arrived(halo_sends[0])

    lifted = dot(pick_halo, ext_halo[0]) + land * land_vec_v[...]
    centred = lifted - jnp.mean(lifted, axis=1, keepdims=True)
    scale = lax.rsqrt(jnp.mean(centred * centred, axis=1, keepdims=True) + 1e-05)
    normed = centred * scale
    normed_f[...] = normed
    projected = dot(normed.astype(BF16), w_qkv_v[...]).astype(BF16)
    for p in range(3 * pairs):
        proj[p] = projected[:, p * 128 : (p + 1) * 128]
    half = lax.broadcasted_iota(jnp.int32, (TOK, 128), 1) < 64
    zero = jnp.zeros((TOK, 128), BF16)

    def both_heads(pair):
        return jnp.concatenate([jnp.where(half, pair, zero), jnp.where(half, zero, pair)], axis=0)

    @pl.loop(0, pairs)
    def _(p):
        weights = jnp.exp(dot(proj[pairs + p], both_heads(proj[p] * 0.125), NT)) * allowed
        att[p] = weights * (1.0 / jnp.sum(weights, axis=0, keepdims=True))

    arrived(halo_sends[1])
    cot_f[...] = dot(pick_halo, ext_halo[1])
    c_out.wait()

    @pl.when(early)
    def _():
        pick = one_hot(read_codes(s_early - s_late, t_early - t_late), codes_v[1:2, : mid.held])
        arrived(mid_sends)
        cot_f[...] += dot(pick, ext_mid[...])

    cot_w = cot_f[...].astype(BF16)

    d_all = dot(cot_w, w_out_v[...], NT).astype(BF16)
    for p in range(pairs):
        d_mixed[p] = d_all[:, p * 128 : (p + 1) * 128]

    @pl.loop(0, pairs, unroll=2)
    def _(p):
        d_both = both_heads(d_mixed[p])
        attention = att[p]
        inner = attention * dot(proj[2 * pairs + p], d_both, NT)
        d_scores = (inner - attention * jnp.sum(inner, axis=0, keepdims=True)).astype(BF16)
        d_query = dot(d_scores, proj[pairs + p], TN)
        d_query = jnp.where(half, d_query[:TOK], d_query[TOK:]) * 0.125
        d_proj[p] = d_query.astype(BF16)
        d_proj[pairs + p] = dot(d_scores, both_heads(proj[p] * 0.125)).astype(BF16)
        d_proj[2 * pairs + p] = dot(attention.astype(BF16), d_both).astype(BF16)

    d_all = jnp.concatenate([d_proj[p] for p in range(3 * pairs)], axis=1)
    d_normed = dot(d_all, w_qkv_v[...], NT).astype(BF16).astype(F32)
    normed = normed_f[...]
    along = jnp.mean(d_normed * normed, axis=1, keepdims=True)
    total = cot_w.astype(F32) + scale * (d_normed - jnp.mean(d_normed, axis=1, keepdims=True) - normed * along)
    ext_out[pl.ds(0, TOK)] = total.astype(BF16)

    @pl.when(late)
    def _():
        mid_sends[0].start()
        send_mid[...] = dot(packing(4, mid), ext_out[pl.ds(0, TOK)], TN).astype(BF16)
        started(mid_sends[1:])
        for copy in mid_sends:
            copy.wait_send()

    send_out[...] = dot(packing(5, out), ext_out[pl.ds(0, TOK)], TN).astype(BF16)
    started(out_sends)
    pick_out = one_hot(read_codes(-s, -t), codes_v[2:3, : out.held])
    arrived(out_sends)
    home = dot(pick_out, ext_out[...]) + direct[...].astype(F32)
    result[...] = home.astype(BF16).reshape(result.shape)

    for copy in halo_sends[0] + halo_sends[1] + out_sends:
        copy.wait_send()


def variant(sizes, number, starts, states, final_cot, step_cot, w_qkv, w_out, land_vec, land_sea, ground, shifts):
    before, after = max(-min(starts), 0), max(max(starts), 0)
    apart = starts[0] - starts[1]
    halo = Exchange(after, before, 5, 6)
    mid = Exchange(max(apart, 0), max(-apart, 0), 6, 6)
    out = Exchange(before, after, 6, 5)
    features = w_qkv.shape[0]
    codes = np.full((8, 512), -1, np.int32)
    for i, e in enumerate((halo, mid, out)):
        codes[i, : e.held] = e.codes
        codes[3 + i, : e.sent] = e.packed
    held_spec = pl.BlockSpec(memory_space=pltpu.HBM)

    def field(*shape):
        return pltpu.VMEM(shape, BF16)

    def home(block):
        return jnp.moveaxis(block, 0, 2).reshape(TOK // LEV, LEV, features)

    gradient = pl.pallas_call(
        functools.partial(kernel, sizes, starts, halo, mid, out),
        out_shape=jax.ShapeDtypeStruct((TOK // LEV, LEV, features), BF16),
        in_specs=[held_spec] * 10,
        out_specs=pl.BlockSpec(memory_space=pltpu.VMEM),
        scratch_shapes=[
            field(3, TOK // LEV, LEV, features),
            field(*w_qkv.shape),
            field(*w_out.shape),
            pltpu.VMEM((1, features), F32),
            pltpu.VMEM((2,) + land_sea.shape, jnp.int32),
            pltpu.SMEM(shifts.shape, jnp.int32),
            pltpu.VMEM(codes.shape, jnp.int32),
            field(2, halo.held, features),
            field(mid.held, features),
            field(out.held, features),
            field(2, halo.sent, features),
            field(mid.sent, features),
            field(out.sent, features),
            pltpu.VMEM((TOK, features), F32),
            field(3 * HEADS // 2, TOK, 128),
            pltpu.VMEM((HEADS // 2, TOK, 2 * TOK), F32),
            pltpu.VMEM((TOK, features), F32),
            field(3 * HEADS // 2, TOK, 128),
            field(HEADS // 2, TOK, 128),
            field(TOK, features),
            pltpu.SemaphoreType.DMA((10,)),
            pltpu.SemaphoreType.DMA((33,)),
            pltpu.SemaphoreType.DMA((33,)),
            pltpu.SemaphoreType.REGULAR,
        ],
        compiler_params=pltpu.CompilerParams(
            collective_id=number, has_side_effects=True, vmem_limit_bytes=60 * 1024 * 1024
        ),
    )(
        home(states[0]), home(final_cot), home(step_cot), w_qkv, w_out, land_vec.reshape(1, features),
        land_sea, ground, shifts, jnp.asarray(codes),
    )
    return jnp.moveaxis(gradient.reshape(WLAT, WLON, LEV, features), 2, 0)[None]


def per_device(sizes, *operands):
    others = (1, 2, 3 - WLAT, 4 - WLAT, -1)
    pairs = [(start, -1) for start in others] + [(-1, start) for start in others[:-1]]
    shifts = operands[-1]
    one, five = np.array([[1, 0], [1, 0]], np.int32), np.array([[0, 0], [5, 0]], np.int32)
    case = jnp.sum((shifts - 3) * one + jnp.minimum(5 - shifts, 1) * five)
    cases = [functools.partial(variant, sizes, number, pair) for number, pair in enumerate(pairs)]
    return lax.switch(case, cases, *operands)


def solution(mesh):
    return jax.shard_map(
        functools.partial(per_device, (mesh.shape["lat"], mesh.shape["lon"])),
        mesh=mesh,
        in_specs=(
            P("step", None, "lat", "lon", None),
            P(None, "lat", "lon", None),
            P(None, "lat", "lon", None),
            P(),
            P(),
            P(),
            P(),
            P(),
            P(),
        ),
        out_specs=P("step", None, "lat", "lon", None),
        check_vma=False,
    )
```

```python
import functools

import jax
import jax.numpy as jnp
import numpy as np
from jax import lax
from jax.experimental import pallas as pl
from jax.experimental.pallas import tpu as pltpu
from jax.sharding import PartitionSpec as P

HEADS = 8
LEV = 2
WLAT = 6
WLON = 12
ROW = WLON * LEV
TOK = WLAT * ROW
MESH = pl.DeviceIdType.MESH
F32 = jnp.float32
BF16 = jnp.bfloat16
NT = (((1,), (1,)), ((), ()))
TN = (((0,), (0,)), ((), ()))


def up_to(value, unit):
    return -(-value // unit) * unit


class Exchange:
    def __init__(self, first_rows, last_rows, first_cols, last_cols):
        rows = {-1: range(first_rows), 0: range(WLAT), 1: range(WLAT - last_rows, WLAT)}
        cols = {-1: range(first_cols), 0: range(WLON), 1: range(WLON - last_cols, WLON)}
        self.pieces = []
        packed, codes = [], list(range(4 * TOK, 5 * TOK))
        offset = 0
        for dy, dx in ((1, 1), (1, -1), (-1, 1), (-1, -1), (1, 0), (-1, 0), (0, 1), (0, -1)):
            tokens = [(r * WLON + c) * LEV + l for r in rows[dy] for c in cols[dx] for l in range(LEV)]
            if not tokens:
                continue
            size = up_to(len(tokens), 16)
            zone = (1 - dy) * 3 + 1 - dx
            filler = [-1] * (size - len(tokens))
            codes += [zone * TOK + token for token in tokens] + filler
            packed += tokens + filler
            self.pieces.append((dy, dx, offset, size))
            offset += size
        self.sent = offset
        self.held = TOK + offset
        self.codes, self.packed = np.array(codes, np.int32), np.array(packed, np.int32)


def quotient(value, by):
    factor = (1 << 14) // by + 1
    assert all((i * factor) >> 14 == i // by for i in range(TOK + 1))
    return (value * factor) >> 14


def frame_places():
    index = lax.broadcasted_iota(jnp.int32, (TOK, 1), 0)
    place = index >> 1
    row = quotient(place, WLON)
    return row, place - row * WLON, index & 1


def read_codes(down, right):
    row, col, level = frame_places()
    row, col = row + down, col + right
    zone_row = jnp.where(row >= WLAT, 1, 0) - jnp.where(row < 0, 1, 0)
    zone_col = jnp.where(col >= WLON, 1, 0) - jnp.where(col < 0, 1, 0)
    place = (row - zone_row * WLAT) * WLON + col - zone_col * WLON
    return ((zone_row + 1) * 3 + zone_col + 1) * TOK + place * LEV + level


def one_hot(left, right):
    return jnp.where(left == right, 1.0, 0.0).astype(BF16)


def dot(a, b, dims=(((1,), (0,)), ((), ()))):
    return lax.dot_general(a, b, dims, preferred_element_type=F32)


def kernel(
    sizes, starts, halo, mid, out,
    states, final_cot, step_cot, w_qkv, w_out, land_vec, land_sea, ground, shifts, codes,
    result,
    raw, w_qkv_v, w_out_v, land_vec_v, tables_v, shifts_v, codes_v,
    ext_halo, ext_mid, ext_out, send_halo, send_mid, send_out, pick_halo, pick_mid, pick_out, pack_mid, pack_out,
    normed_f, proj, att, cot_f, d_proj, d_mixed, direct,
    local_sem, send_sem, recv_sem, go_sem,
):
    n_lat, n_lon = sizes
    features = w_qkv.shape[0]
    quads = HEADS // 4
    wide = features // quads
    step, lat, lon = lax.axis_index("step"), lax.axis_index("lat"), lax.axis_index("lon")
    late = step == 1
    early = step == 0

    def around(dy, dx, other=False):
        return (
            1 - step if other else step,
            lax.rem(lat + (dy + n_lat), n_lat),
            lax.rem(lon + (dx + n_lon), n_lon),
        )

    to_early = [(0, 0)] + [(dy, dx) for dy, dx, _, _ in mid.pieces]
    to_same = sorted(
        {(dy * k, dx * k) for e in halo + out for dy, dx, _, _ in e.pieces for k in (1, -1)}
    )
    sign = 2 * step - 1
    barrier = pltpu.get_barrier_semaphore()
    for dy, dx in to_same:
        pl.semaphore_signal(barrier, inc=1, device_id=around(dy, dx), device_id_type=MESH)
    for dy, dx in to_early:
        pl.semaphore_signal(barrier, inc=1, device_id=around(dy * sign, dx * sign, True), device_id_type=MESH)

    local = [
        pltpu.make_async_copy(src, dst, local_sem.at[i])
        for i, (src, dst) in enumerate((
            (states, raw.at[0]),
            (codes, codes_v),
            (step_cot, raw.at[2]),
            (shifts, shifts_v),
            (land_sea, tables_v.at[0]),
            (ground, tables_v.at[1]),
            (land_vec, land_vec_v),
            (w_qkv, w_qkv_v),
            (w_out, w_out_v),
            (final_cot, raw.at[1]),
        ))
    ]
    (c_state, c_codes, c_step, c_shift, c_land, c_ground, c_vec, c_qkv, c_out, c_final) = local
    for copy in local:
        copy.start()

    def remotes(first, exchange, src, dst, other=False):
        return [
            pltpu.make_async_remote_copy(
                src_ref=src.at[pl.ds(offset, size)], dst_ref=dst.at[pl.ds(TOK + offset, size)],
                send_sem=send_sem.at[first + k], recv_sem=recv_sem.at[first + k],
                device_id=around(dy, dx, other), device_id_type=MESH,
            )
            for k, (dy, dx, offset, size) in enumerate(exchange.pieces)
        ]

    halo_sends = [[remotes(8 * i, halo[half], send_halo.at[i], ext_halo.at[i]) for i in range(2)] for half in range(2)]
    out_sends = [remotes(16, out[half], send_out, ext_out) for half in range(2)]
    mid_sends = [pltpu.make_async_remote_copy(
        src_ref=ext_out.at[pl.ds(0, TOK)], dst_ref=ext_mid.at[pl.ds(0, TOK)],
        send_sem=send_sem.at[32], recv_sem=recv_sem.at[32], device_id=around(0, 0, True), device_id_type=MESH,
    )] + remotes(24, mid, send_mid, ext_mid, True)

    def started(copies):
        for copy in copies:
            copy.start()

    def arrived(copies):
        for copy in copies:
            copy.wait_recv()

    def own_row(first, width):
        return jnp.where(late, codes_v[first + 1 : first + 2, :width], codes_v[first : first + 1, :width])

    def packing(row):
        token = lax.broadcasted_iota(jnp.int32, (TOK, row.shape[1]), 0)
        same = lax.broadcasted_iota(jnp.int32, (TOK, TOK), 0) == lax.broadcasted_iota(jnp.int32, (TOK, TOK), 1)
        return dot(one_hot(token, row), jnp.where(same, 1.0, 0.0).astype(BF16), TN).astype(BF16)

    def clear(target, exchange):
        rows = target.shape[0] - exchange.held
        if rows:
            target[pl.ds(exchange.held, rows)] = jnp.zeros((rows, features), BF16)

    c_codes.wait()
    pack_halo = packing(own_row(8, send_halo.shape[1]))
    c_state.wait()
    c_step.wait()
    c_final.wait()
    ext_halo[0, pl.ds(0, TOK)] = raw[0].reshape(TOK, features)
    send_halo[0] = dot(pack_halo, ext_halo[0, pl.ds(0, TOK)]).astype(BF16)
    pl.semaphore_wait(barrier, len(to_same) + len(to_early))

    @pl.when(late)
    def _():
        started(halo_sends[1][0])

    ext_halo[1, pl.ds(0, TOK)] = raw[2 - step].reshape(TOK, features)
    send_halo[1] = dot(pack_halo, ext_halo[1, pl.ds(0, TOK)]).astype(BF16)

    @pl.when(late)
    def _():
        direct[...] = raw[2].reshape(TOK, features)
        clear(ext_halo.at[0], halo[1])
        clear(ext_halo.at[1], halo[1])
        clear(ext_out, out[1])

    @pl.when(early)
    def _():
        direct[...] = jnp.zeros((TOK, features), BF16)
        clear(ext_halo.at[0], halo[0])
        clear(ext_halo.at[1], halo[0])
        clear(ext_out, out[0])

    c_shift.wait()
    s_early, s_late = starts
    t_early, t_late = (jnp.where(b >= 6, b - WLON, b) for b in (shifts_v[0, 1], shifts_v[1, 1]))
    s = jnp.where(late, s_late, s_early)
    t = jnp.where(late, t_late, t_early)
    pick_halo[...] = one_hot(read_codes(s, t), own_row(0, ext_halo.shape[1]))
    pick_out[...] = one_hot(read_codes(-s, -t), own_row(3, ext_out.shape[0]))
    pack_out[...] = packing(own_row(11, send_out.shape[0]))
    pack_mid[...] = packing(codes_v[10:11, : mid.sent])
    pick_mid[...] = one_hot(read_codes(s_early - s_late, t_early - t_late), codes_v[2:3, : mid.held])

    row, col, level = frame_places()
    lat_total, lon_total = tables_v.shape[1], tables_v.shape[2]
    at_row = lat * WLAT + s + row
    at_row = jnp.where(at_row < 0, at_row + lat_total, jnp.where(at_row >= lat_total, at_row - lat_total, at_row))
    at_col = lon * WLON + t + col
    at_col = jnp.where(at_col < 0, at_col + lon_total, jnp.where(at_col >= lon_total, at_col - lon_total, at_col))
    c_land.wait()
    c_ground.wait()
    row_pick = one_hot(at_row, lax.broadcasted_iota(jnp.int32, (TOK, lat_total), 1))
    col_pick = at_col == lax.broadcasted_iota(jnp.int32, (TOK, lon_total), 1)

    def looked_up(table):
        lines = dot(row_pick, table.astype(F32).astype(BF16))
        return jnp.sum(jnp.where(col_pick, lines, 0.0), axis=1, keepdims=True)

    both = looked_up(tables_v[0] + 2 * tables_v[1])
    ground_at = jnp.where(both >= 1.5, 1.0, 0.0)
    land = both - 2.0 * ground_at
    key_valid = jnp.where(level.astype(F32) >= ground_at, 1.0, 0.0)
    shift_lat = jnp.where(s < 0, s + WLAT, s)
    window = jnp.where(s < 0, lax.rem(lat + (n_lat - 1), n_lat), lat)
    first_seam = jnp.where(window == n_lat - 1, WLAT - shift_lat, WLAT)
    lane = lax.broadcasted_iota(jnp.int32, (1, 4 * TOK), 1)
    lane = jnp.where(lane >= 2 * TOK, lane - 2 * TOK, lane)
    lane = jnp.where(lane >= TOK, lane - TOK, lane)
    seam_key = jnp.where(row >= first_seam, 1, 0)
    seam_query = jnp.where(quotient(lane >> 1, WLON) >= first_seam, 1, 0)
    allowed = jnp.where(seam_key == seam_query, key_valid, 0.0)
    c_vec.wait()
    c_qkv.wait()

    @pl.when(late)
    def _():
        started(halo_sends[1][1])
        arrived(halo_sends[1][0])
        pl.semaphore_signal(go_sem, inc=1, device_id=around(0, 0, True), device_id_type=MESH)

    @pl.when(early)
    def _():
        pl.semaphore_wait(go_sem, 1)
        started(halo_sends[0][0] + halo_sends[0][1])
        arrived(halo_sends[0][0])

    lifted = dot(pick_halo[...], ext_halo[0]) + land * land_vec_v[...]
    centred = lifted - jnp.mean(lifted, axis=1, keepdims=True)
    scale = lax.rsqrt(jnp.mean(centred * centred, axis=1, keepdims=True) + 1e-05)
    normed = centred * scale
    normed_f[...] = normed
    projected = dot(normed.astype(BF16), w_qkv_v[...]).astype(BF16)
    for p in range(3 * quads):
        proj[p] = projected[:, p * wide : (p + 1) * wide]
    group = lax.broadcasted_iota(jnp.int32, (TOK, wide), 1) >> 6
    zero = jnp.zeros((TOK, wide), BF16)

    def by_head(quad):
        return jnp.concatenate([jnp.where(group == h, quad, zero) for h in range(4)], axis=0)

    @pl.loop(0, quads)
    def _(p):
        weights = jnp.exp(dot(proj[quads + p], by_head(proj[p] * 0.125), NT)) * allowed
        att[p] = weights * (1.0 / jnp.sum(weights, axis=0, keepdims=True))

    @pl.when(late)
    def _():
        arrived(halo_sends[1][1])

    @pl.when(early)
    def _():
        arrived(halo_sends[0][1])

    cot_f[...] = dot(pick_halo[...], ext_halo[1])
    c_out.wait()

    @pl.when(early)
    def _():
        arrived(mid_sends)
        cot_f[...] += dot(pick_mid[...], ext_mid[...])

    cot_w = cot_f[...].astype(BF16)

    d_all = dot(cot_w, w_out_v[...], NT).astype(BF16)
    for p in range(quads):
        d_mixed[p] = d_all[:, p * wide : (p + 1) * wide]

    @pl.loop(0, quads)
    def _(p):
        d_heads = by_head(d_mixed[p])
        attention = att[p]
        inner = attention * dot(proj[2 * quads + p], d_heads, NT)
        d_scores = (inner - attention * jnp.sum(inner, axis=0, keepdims=True)).astype(BF16)
        d_each = dot(d_scores, proj[quads + p], TN)
        d_query = d_each[:TOK]
        for h in range(1, 4):
            d_query = jnp.where(group == h, d_each[h * TOK : (h + 1) * TOK], d_query)
        d_proj[p] = (d_query * 0.125).astype(BF16)
        d_proj[quads + p] = dot(d_scores, by_head(proj[p] * 0.125)).astype(BF16)
        d_proj[2 * quads + p] = dot(attention.astype(BF16), d_heads).astype(BF16)

    d_all = jnp.concatenate([d_proj[p] for p in range(3 * quads)], axis=1)
    d_normed = dot(d_all, w_qkv_v[...], NT).astype(BF16).astype(F32)
    normed = normed_f[...]
    along = jnp.mean(d_normed * normed, axis=1, keepdims=True)
    total = cot_w.astype(F32) + scale * (d_normed - jnp.mean(d_normed, axis=1, keepdims=True) - normed * along)
    ext_out[pl.ds(0, TOK)] = total.astype(BF16)

    @pl.when(late)
    def _():
        mid_sends[0].start()
        send_mid[...] = dot(pack_mid[...], ext_out[pl.ds(0, TOK)]).astype(BF16)
        started(mid_sends[1:])
        for copy in mid_sends:
            copy.wait_send()

    send_out[...] = dot(pack_out[...], ext_out[pl.ds(0, TOK)]).astype(BF16)

    @pl.when(late)
    def _():
        started(out_sends[1])
        arrived(out_sends[1])

    @pl.when(early)
    def _():
        started(out_sends[0])
        arrived(out_sends[0])

    home = dot(pick_out[...], ext_out[...]) + direct[...].astype(F32)
    result[...] = home.astype(BF16).reshape(result.shape)

    @pl.when(late)
    def _():
        for copy in halo_sends[1][0] + halo_sends[1][1] + out_sends[1]:
            copy.wait_send()

    @pl.when(early)
    def _():
        for copy in halo_sends[0][0] + halo_sends[0][1] + out_sends[0]:
            copy.wait_send()


def variant(sizes, number, starts, states, final_cot, step_cot, w_qkv, w_out, land_vec, land_sea, ground, shifts):
    before, after = [max(-start, 0) for start in starts], [max(start, 0) for start in starts]
    apart = starts[0] - starts[1]
    halo = [Exchange(after[half], before[half], 5, 6) for half in range(2)]
    mid = Exchange(max(apart, 0), max(-apart, 0), 6, 6)
    out = [Exchange(before[half], after[half], 6, 5) for half in range(2)]
    features = w_qkv.shape[0]
    codes = np.full((16, 512), -1, np.int32)
    for i, e in enumerate(halo + [mid] + out):
        codes[i, : e.held] = e.codes
        codes[8 + i, : e.sent] = e.packed
    halo_held, halo_sent = max(e.held for e in halo), max(e.sent for e in halo)
    out_held, out_sent = max(e.held for e in out), max(e.sent for e in out)
    held_spec = pl.BlockSpec(memory_space=pltpu.HBM)

    def field(*shape):
        return pltpu.VMEM(shape, BF16)

    def home(block):
        return jnp.moveaxis(block, 0, 2).reshape(TOK // LEV, LEV, features)

    gradient = pl.pallas_call(
        functools.partial(kernel, sizes, starts, halo, mid, out),
        out_shape=jax.ShapeDtypeStruct((TOK // LEV, LEV, features), BF16),
        in_specs=[held_spec] * 10,
        out_specs=pl.BlockSpec(memory_space=pltpu.VMEM),
        scratch_shapes=[
            field(3, TOK // LEV, LEV, features),
            field(*w_qkv.shape),
            field(*w_out.shape),
            pltpu.VMEM((1, features), F32),
            pltpu.VMEM((2,) + land_sea.shape, jnp.int32),
            pltpu.SMEM(shifts.shape, jnp.int32),
            pltpu.VMEM(codes.shape, jnp.int32),
            field(2, halo_held, features),
            field(mid.held, features),
            field(out_held, features),
            field(2, halo_sent, features),
            field(mid.sent, features),
            field(out_sent, features),
            field(TOK, halo_held),
            field(TOK, mid.held),
            field(TOK, out_held),
            field(mid.sent, TOK),
            field(out_sent, TOK),
            pltpu.VMEM((TOK, features), F32),
            field(3 * HEADS // 4, TOK, 4 * features // HEADS),
            pltpu.VMEM((HEADS // 4, TOK, 4 * TOK), F32),
            pltpu.VMEM((TOK, features), F32),
            field(3 * HEADS // 4, TOK, 4 * features // HEADS),
            field(HEADS // 4, TOK, 4 * features // HEADS),
            field(TOK, features),
            pltpu.SemaphoreType.DMA((10,)),
            pltpu.SemaphoreType.DMA((33,)),
            pltpu.SemaphoreType.DMA((33,)),
            pltpu.SemaphoreType.REGULAR,
        ],
        compiler_params=pltpu.CompilerParams(
            collective_id=number, has_side_effects=True, vmem_limit_bytes=60 * 1024 * 1024
        ),
    )(
        home(states[0]), home(final_cot), home(step_cot), w_qkv, w_out, land_vec.reshape(1, features),
        land_sea, ground, shifts, jnp.asarray(codes),
    )
    return jnp.moveaxis(gradient.reshape(WLAT, WLON, LEV, features), 2, 0)[None]


def per_device(sizes, *operands):
    others = (1, 2, 3 - WLAT, 4 - WLAT, -1)
    pairs = [(start, -1) for start in others] + [(-1, start) for start in others[:-1]]
    shifts = operands[-1]
    one, five = np.array([[1, 0], [1, 0]], np.int32), np.array([[0, 0], [5, 0]], np.int32)
    case = jnp.sum((shifts - 3) * one + jnp.minimum(5 - shifts, 1) * five)
    cases = [functools.partial(variant, sizes, number, pair) for number, pair in enumerate(pairs)]
    return lax.switch(case, cases, *operands)


def solution(mesh):
    return jax.shard_map(
        functools.partial(per_device, (mesh.shape["lat"], mesh.shape["lon"])),
        mesh=mesh,
        in_specs=(
            P("step", None, "lat", "lon", None),
            P(None, "lat", "lon", None),
            P(None, "lat", "lon", None),
            P(),
            P(),
            P(),
            P(),
            P(),
            P(),
        ),
        out_specs=P("step", None, "lat", "lon", None),
        check_vma=False,
    )
```

```python
import functools

import jax
import jax.numpy as jnp
import numpy as np
from jax import lax
from jax.experimental import pallas as pl
from jax.experimental.pallas import tpu as pltpu
from jax.sharding import PartitionSpec as P

HEADS = 8
LEV = 2
WLAT = 6
WLON = 12
ROW = WLON * LEV
TOK = WLAT * ROW
MESH = pl.DeviceIdType.MESH
F32 = jnp.float32
BF16 = jnp.bfloat16
NT = (((1,), (1,)), ((), ()))
TN = (((0,), (0,)), ((), ()))


def up_to(value, unit):
    return -(-value // unit) * unit


class Exchange:
    def __init__(self, first_rows, last_rows, first_cols, last_cols):
        rows = {-1: range(first_rows), 0: range(WLAT), 1: range(WLAT - last_rows, WLAT)}
        cols = {-1: range(first_cols), 0: range(WLON), 1: range(WLON - last_cols, WLON)}
        self.pieces = []
        packed, codes = [], list(range(4 * TOK, 5 * TOK))
        offset = 0
        for dy, dx in ((1, 1), (1, -1), (-1, 1), (-1, -1), (1, 0), (-1, 0), (0, 1), (0, -1)):
            tokens = [(r * WLON + c) * LEV + l for r in rows[dy] for c in cols[dx] for l in range(LEV)]
            if not tokens:
                continue
            size = up_to(len(tokens), 16)
            zone = (1 - dy) * 3 + 1 - dx
            filler = [-1] * (size - len(tokens))
            codes += [zone * TOK + token for token in tokens] + filler
            packed += tokens + filler
            self.pieces.append((dy, dx, offset, size))
            offset += size
        self.sent = offset
        self.held = TOK + offset
        self.codes, self.packed = np.array(codes, np.int32), np.array(packed, np.int32)


def quotient(value, by):
    factor = (1 << 14) // by + 1
    assert all((i * factor) >> 14 == i // by for i in range(TOK + 1))
    return (value * factor) >> 14


def frame_places():
    index = lax.broadcasted_iota(jnp.int32, (TOK, 1), 0)
    place = index >> 1
    row = quotient(place, WLON)
    return row, place - row * WLON, index & 1


def read_codes(down, right):
    row, col, level = frame_places()
    row, col = row + down, col + right
    zone_row = jnp.where(row >= WLAT, 1, 0) - jnp.where(row < 0, 1, 0)
    zone_col = jnp.where(col >= WLON, 1, 0) - jnp.where(col < 0, 1, 0)
    place = (row - zone_row * WLAT) * WLON + col - zone_col * WLON
    return ((zone_row + 1) * 3 + zone_col + 1) * TOK + place * LEV + level


def one_hot(left, right):
    return jnp.where(left == right, 1.0, 0.0).astype(BF16)


def dot(a, b, dims=(((1,), (0,)), ((), ()))):
    return lax.dot_general(a, b, dims, preferred_element_type=F32)


def kernel(
    sizes, starts, halo, mid, out,
    states, final_cot, step_cot, w_qkv, w_out, land_vec, land_sea, ground, shifts, codes,
    result,
    raw, w_qkv_v, w_out_v, land_vec_v, tables_v, shifts_v, codes_v,
    ext_halo, ext_mid, ext_out, send_halo, send_mid, send_out, pick_halo, pick_mid, pick_out, pick_own, pack_mid, pack_out,
    normed_f, proj, att, cot_f, d_proj, d_mixed, direct,
    local_sem, send_sem, recv_sem, go_sem,
):
    n_lat, n_lon = sizes
    features = w_qkv.shape[0]
    quads = HEADS // 4
    wide = features // quads
    step, lat, lon = lax.axis_index("step"), lax.axis_index("lat"), lax.axis_index("lon")
    late = step == 1
    early = step == 0

    def around(dy, dx, other=False):
        return (
            1 - step if other else step,
            lax.rem(lat + (dy + n_lat), n_lat),
            lax.rem(lon + (dx + n_lon), n_lon),
        )

    to_early = [(0, 0)] + [(dy, dx) for dy, dx, _, _ in mid.pieces]
    to_same = sorted(
        {(dy * k, dx * k) for e in halo + out for dy, dx, _, _ in e.pieces for k in (1, -1)}
    )
    sign = 2 * step - 1
    barrier = pltpu.get_barrier_semaphore()
    for dy, dx in to_same:
        pl.semaphore_signal(barrier, inc=1, device_id=around(dy, dx), device_id_type=MESH)
    for dy, dx in to_early:
        pl.semaphore_signal(barrier, inc=1, device_id=around(dy * sign, dx * sign, True), device_id_type=MESH)

    local = [
        pltpu.make_async_copy(src, dst, local_sem.at[i])
        for i, (src, dst) in enumerate((
            (states, raw.at[0]),
            (codes, codes_v),
            (step_cot, raw.at[2]),
            (shifts, shifts_v),
            (land_sea, tables_v.at[0]),
            (ground, tables_v.at[1]),
            (land_vec, land_vec_v),
            (w_qkv, w_qkv_v),
            (w_out, w_out_v),
            (final_cot, raw.at[1]),
        ))
    ]
    (c_state, c_codes, c_step, c_shift, c_land, c_ground, c_vec, c_qkv, c_out, c_final) = local
    for copy in local:
        copy.start()

    def remotes(first, exchange, src, dst, other=False):
        return [
            pltpu.make_async_remote_copy(
                src_ref=src.at[pl.ds(offset, size)], dst_ref=dst.at[pl.ds(TOK + offset, size)],
                send_sem=send_sem.at[first + k], recv_sem=recv_sem.at[first + k],
                device_id=around(dy, dx, other), device_id_type=MESH,
            )
            for k, (dy, dx, offset, size) in enumerate(exchange.pieces)
        ]

    halo_sends = [[remotes(8 * i, halo[half], send_halo.at[i], ext_halo.at[i]) for i in range(2)] for half in range(2)]
    out_sends = [remotes(16, out[half], send_out, ext_out) for half in range(2)]
    mid_sends = [pltpu.make_async_remote_copy(
        src_ref=ext_out.at[pl.ds(0, TOK)], dst_ref=ext_mid.at[pl.ds(0, TOK)],
        send_sem=send_sem.at[32], recv_sem=recv_sem.at[32], device_id=around(0, 0, True), device_id_type=MESH,
    )] + remotes(24, mid, send_mid, ext_mid, True)

    def started(copies):
        for copy in copies:
            copy.start()

    def arrived(copies):
        for copy in copies:
            copy.wait_recv()

    def own_row(first, width):
        return jnp.where(late, codes_v[first + 1 : first + 2, :width], codes_v[first : first + 1, :width])

    def packing(row):
        token = lax.broadcasted_iota(jnp.int32, (TOK, row.shape[1]), 0)
        same = lax.broadcasted_iota(jnp.int32, (TOK, TOK), 0) == lax.broadcasted_iota(jnp.int32, (TOK, TOK), 1)
        return dot(one_hot(token, row), jnp.where(same, 1.0, 0.0).astype(BF16), TN).astype(BF16)

    def clear(target, exchange):
        rows = target.shape[0] - exchange.held
        if rows:
            target[pl.ds(exchange.held, rows)] = jnp.zeros((rows, features), BF16)

    c_codes.wait()
    pack_halo = packing(own_row(8, send_halo.shape[1]))
    c_state.wait()
    ext_halo[0, pl.ds(0, TOK)] = raw[0].reshape(TOK, features)
    send_halo[0] = dot(pack_halo, ext_halo[0, pl.ds(0, TOK)]).astype(BF16)
    pl.semaphore_wait(barrier, len(to_same) + len(to_early))

    @pl.when(late)
    def _():
        started(halo_sends[1][0])

    c_step.wait()
    c_final.wait()
    ext_halo[1, pl.ds(0, TOK)] = raw[2 - step].reshape(TOK, features)
    send_halo[1] = dot(pack_halo, ext_halo[1, pl.ds(0, TOK)]).astype(BF16)

    @pl.when(late)
    def _():
        direct[...] = raw[2].reshape(TOK, features)
        clear(ext_halo.at[0], halo[1])
        clear(ext_halo.at[1], halo[1])
        clear(ext_out, out[1])

    @pl.when(early)
    def _():
        direct[...] = jnp.zeros((TOK, features), BF16)
        clear(ext_halo.at[0], halo[0])
        clear(ext_halo.at[1], halo[0])
        clear(ext_out, out[0])

    c_shift.wait()
    s_early, s_late = starts
    t_early, t_late = (jnp.where(b >= 6, b - WLON, b) for b in (shifts_v[0, 1], shifts_v[1, 1]))
    s = jnp.where(late, s_late, s_early)
    t = jnp.where(late, t_late, t_early)
    own_codes = lax.broadcasted_iota(jnp.int32, (1, TOK), 1) + 4 * TOK
    read_halo, read_out = read_codes(s, t), read_codes(-s, -t)
    read_mid = read_codes(s_early - s_late, t_early - t_late)
    pick_own[0] = one_hot(read_halo, own_codes)
    pick_own[1] = one_hot(read_mid, own_codes)
    pick_own[2] = one_hot(read_out, own_codes)
    pick_halo[...] = one_hot(read_halo, own_row(0, ext_halo.shape[1] - TOK))
    pick_out[...] = one_hot(read_out, own_row(3, ext_out.shape[0] - TOK))
    pack_out[...] = packing(own_row(11, send_out.shape[0]))
    pack_mid[...] = packing(codes_v[10:11, : mid.sent])
    pick_mid[...] = one_hot(read_mid, codes_v[2:3, : mid.sent])

    row, col, level = frame_places()
    lat_total, lon_total = tables_v.shape[1], tables_v.shape[2]
    at_row = lat * WLAT + s + row
    at_row = jnp.where(at_row < 0, at_row + lat_total, jnp.where(at_row >= lat_total, at_row - lat_total, at_row))
    at_col = lon * WLON + t + col
    at_col = jnp.where(at_col < 0, at_col + lon_total, jnp.where(at_col >= lon_total, at_col - lon_total, at_col))
    c_land.wait()
    c_ground.wait()
    row_pick = one_hot(at_row, lax.broadcasted_iota(jnp.int32, (TOK, lat_total), 1))
    col_pick = at_col == lax.broadcasted_iota(jnp.int32, (TOK, lon_total), 1)

    def looked_up(table):
        lines = dot(row_pick, table.astype(F32).astype(BF16))
        return jnp.sum(jnp.where(col_pick, lines, 0.0), axis=1, keepdims=True)

    both = looked_up(tables_v[0] + 2 * tables_v[1])
    ground_at = jnp.where(both >= 1.5, 1.0, 0.0)
    land = both - 2.0 * ground_at
    key_valid = jnp.where(level.astype(F32) >= ground_at, 1.0, 0.0)
    shift_lat = jnp.where(s < 0, s + WLAT, s)
    window = jnp.where(s < 0, lax.rem(lat + (n_lat - 1), n_lat), lat)
    first_seam = jnp.where(window == n_lat - 1, WLAT - shift_lat, WLAT)
    lane = lax.broadcasted_iota(jnp.int32, (1, 4 * TOK), 1)
    lane = jnp.where(lane >= 2 * TOK, lane - 2 * TOK, lane)
    lane = jnp.where(lane >= TOK, lane - TOK, lane)
    seam_key = jnp.where(row >= first_seam, 1, 0)
    seam_query = jnp.where(quotient(lane >> 1, WLON) >= first_seam, 1, 0)
    allowed = jnp.where(seam_key == seam_query, key_valid, 0.0)
    c_vec.wait()
    c_qkv.wait()

    def picked_own(i, held):
        return dot(pick_own[i], held[pl.ds(0, TOK)])

    def picked(pick, held):
        return dot(pick[...], held[pl.ds(TOK, pick.shape[1])])

    normed_f[...] = picked_own(0, ext_halo.at[0]) + land * land_vec_v[...]
    cot_f[...] = picked_own(0, ext_halo.at[1])

    @pl.when(late)
    def _():
        started(halo_sends[1][1])
        arrived(halo_sends[1][0])
        pl.semaphore_signal(go_sem, inc=1, device_id=around(0, 0, True), device_id_type=MESH)

    @pl.when(early)
    def _():
        pl.semaphore_wait(go_sem, 1)
        started(halo_sends[0][0] + halo_sends[0][1])
        arrived(halo_sends[0][0])

    lifted = normed_f[...] + picked(pick_halo, ext_halo.at[0])
    centred = lifted - jnp.mean(lifted, axis=1, keepdims=True)
    scale = lax.rsqrt(jnp.mean(centred * centred, axis=1, keepdims=True) + 1e-05)
    normed = centred * scale
    normed_f[...] = normed
    projected = dot(normed.astype(BF16), w_qkv_v[...]).astype(BF16)
    for p in range(3 * quads):
        proj[p] = projected[:, p * wide : (p + 1) * wide]
    group = lax.broadcasted_iota(jnp.int32, (TOK, wide), 1) >> 6
    zero = jnp.zeros((TOK, wide), BF16)

    def by_head(quad):
        return jnp.concatenate([jnp.where(group == h, quad, zero) for h in range(4)], axis=0)

    @pl.loop(0, quads, unroll=True)
    def _(p):
        weights = jnp.exp(dot(proj[quads + p], by_head(proj[p] * 0.125), NT)) * allowed
        att[p] = weights * (1.0 / jnp.sum(weights, axis=0, keepdims=True))

    @pl.when(late)
    def _():
        arrived(halo_sends[1][1])

    @pl.when(early)
    def _():
        arrived(halo_sends[0][1])

    cot_f[...] += picked(pick_halo, ext_halo.at[1])
    c_out.wait()

    @pl.when(early)
    def _():
        arrived(mid_sends[:1])
        cot_f[...] += picked_own(1, ext_mid)
        arrived(mid_sends[1:])
        cot_f[...] += picked(pick_mid, ext_mid)

    cot_w = cot_f[...].astype(BF16)

    d_all = dot(cot_w, w_out_v[...], NT).astype(BF16)
    for p in range(quads):
        d_mixed[p] = d_all[:, p * wide : (p + 1) * wide]

    @pl.loop(0, quads, unroll=True)
    def _(p):
        d_heads = by_head(d_mixed[p])
        attention = att[p]
        inner = attention * dot(proj[2 * quads + p], d_heads, NT)
        d_scores = (inner - attention * jnp.sum(inner, axis=0, keepdims=True)).astype(BF16)
        d_each = dot(d_scores, proj[quads + p], TN)
        d_query = d_each[:TOK]
        for h in range(1, 4):
            d_query = jnp.where(group == h, d_each[h * TOK : (h + 1) * TOK], d_query)
        d_proj[p] = (d_query * 0.125).astype(BF16)
        d_proj[quads + p] = dot(d_scores, by_head(proj[p] * 0.125)).astype(BF16)
        d_proj[2 * quads + p] = dot(attention.astype(BF16), d_heads).astype(BF16)

    d_all = jnp.concatenate([d_proj[p] for p in range(3 * quads)], axis=1)
    d_normed = dot(d_all, w_qkv_v[...], NT).astype(BF16).astype(F32)
    normed = normed_f[...]
    along = jnp.mean(d_normed * normed, axis=1, keepdims=True)
    total = cot_w.astype(F32) + scale * (d_normed - jnp.mean(d_normed, axis=1, keepdims=True) - normed * along)
    ext_out[pl.ds(0, TOK)] = total.astype(BF16)

    @pl.when(late)
    def _():
        mid_sends[0].start()
        send_mid[...] = dot(pack_mid[...], ext_out[pl.ds(0, TOK)]).astype(BF16)
        started(mid_sends[1:])
        for copy in mid_sends:
            copy.wait_send()

    send_out[...] = dot(pack_out[...], ext_out[pl.ds(0, TOK)]).astype(BF16)

    @pl.when(late)
    def _():
        started(out_sends[1])

    @pl.when(early)
    def _():
        started(out_sends[0])

    normed_f[...] = picked_own(2, ext_out) + direct[...].astype(F32)

    @pl.when(late)
    def _():
        arrived(out_sends[1])

    @pl.when(early)
    def _():
        arrived(out_sends[0])

    home = normed_f[...] + picked(pick_out, ext_out)
    result[...] = home.astype(BF16).reshape(result.shape)

    @pl.when(late)
    def _():
        for copy in halo_sends[1][0] + halo_sends[1][1] + out_sends[1]:
            copy.wait_send()

    @pl.when(early)
    def _():
        for copy in halo_sends[0][0] + halo_sends[0][1] + out_sends[0]:
            copy.wait_send()


def variant(sizes, number, starts, states, final_cot, step_cot, w_qkv, w_out, land_vec, land_sea, ground, shifts):
    before, after = [max(-start, 0) for start in starts], [max(start, 0) for start in starts]
    apart = starts[0] - starts[1]
    halo = [Exchange(after[half], before[half], 5, 6) for half in range(2)]
    mid = Exchange(max(apart, 0), max(-apart, 0), 6, 6)
    out = [Exchange(before[half], after[half], 6, 5) for half in range(2)]
    features = w_qkv.shape[0]
    codes = np.full((16, 512), -1, np.int32)
    for i, e in enumerate(halo + [mid] + out):
        codes[i, : e.sent] = e.codes[TOK:]
        codes[8 + i, : e.sent] = e.packed
    halo_held, halo_sent = max(e.held for e in halo), max(e.sent for e in halo)
    out_held, out_sent = max(e.held for e in out), max(e.sent for e in out)
    held_spec = pl.BlockSpec(memory_space=pltpu.HBM)

    def field(*shape):
        return pltpu.VMEM(shape, BF16)

    def home(block):
        return jnp.moveaxis(block, 0, 2).reshape(TOK // LEV, LEV, features)

    gradient = pl.pallas_call(
        functools.partial(kernel, sizes, starts, halo, mid, out),
        out_shape=jax.ShapeDtypeStruct((TOK // LEV, LEV, features), BF16),
        in_specs=[held_spec] * 10,
        out_specs=pl.BlockSpec(memory_space=pltpu.VMEM),
        scratch_shapes=[
            field(3, TOK // LEV, LEV, features),
            field(*w_qkv.shape),
            field(*w_out.shape),
            pltpu.VMEM((1, features), F32),
            pltpu.VMEM((2,) + land_sea.shape, jnp.int32),
            pltpu.SMEM(shifts.shape, jnp.int32),
            pltpu.VMEM(codes.shape, jnp.int32),
            field(2, halo_held, features),
            field(mid.held, features),
            field(out_held, features),
            field(2, halo_sent, features),
            field(mid.sent, features),
            field(out_sent, features),
            field(TOK, halo_sent),
            field(TOK, mid.sent),
            field(TOK, out_sent),
            field(3, TOK, TOK),
            field(mid.sent, TOK),
            field(out_sent, TOK),
            pltpu.VMEM((TOK, features), F32),
            field(3 * HEADS // 4, TOK, 4 * features // HEADS),
            pltpu.VMEM((HEADS // 4, TOK, 4 * TOK), F32),
            pltpu.VMEM((TOK, features), F32),
            field(3 * HEADS // 4, TOK, 4 * features // HEADS),
            field(HEADS // 4, TOK, 4 * features // HEADS),
            field(TOK, features),
            pltpu.SemaphoreType.DMA((10,)),
            pltpu.SemaphoreType.DMA((33,)),
            pltpu.SemaphoreType.DMA((33,)),
            pltpu.SemaphoreType.REGULAR,
        ],
        compiler_params=pltpu.CompilerParams(
            collective_id=number, has_side_effects=True, vmem_limit_bytes=60 * 1024 * 1024
        ),
    )(
        home(states[0]), home(final_cot), home(step_cot), w_qkv, w_out, land_vec.reshape(1, features),
        land_sea, ground, shifts, jnp.asarray(codes),
    )
    return jnp.moveaxis(gradient.reshape(WLAT, WLON, LEV, features), 2, 0)[None]


def per_device(sizes, *operands):
    others = (1, 2, 3 - WLAT, 4 - WLAT, -1)
    pairs = [(start, -1) for start in others] + [(-1, start) for start in others[:-1]]
    shifts = operands[-1]
    one, five = np.array([[1, 0], [1, 0]], np.int32), np.array([[0, 0], [5, 0]], np.int32)
    case = jnp.sum((shifts - 3) * one + jnp.minimum(5 - shifts, 1) * five)
    cases = [functools.partial(variant, sizes, number, pair) for number, pair in enumerate(pairs)]
    return lax.switch(case, cases, *operands)


def solution(mesh):
    return jax.shard_map(
        functools.partial(per_device, (mesh.shape["lat"], mesh.shape["lon"])),
        mesh=mesh,
        in_specs=(
            P("step", None, "lat", "lon", None),
            P(None, "lat", "lon", None),
            P(None, "lat", "lon", None),
            P(),
            P(),
            P(),
            P(),
            P(),
            P(),
        ),
        out_specs=P("step", None, "lat", "lon", None),
        check_vma=False,
    )
```

```python
import functools

import jax
import jax.numpy as jnp
import numpy as np
from jax import lax
from jax.experimental import pallas as pl
from jax.experimental.pallas import tpu as pltpu
from jax.sharding import PartitionSpec as P

HEADS = 8
LEV = 2
WLAT = 6
WLON = 12
ROW = WLON * LEV
TOK = WLAT * ROW
MESH = pl.DeviceIdType.MESH
F32 = jnp.float32
BF16 = jnp.bfloat16
NT = (((1,), (1,)), ((), ()))
TN = (((0,), (0,)), ((), ()))


def up_to(value, unit):
    return -(-value // unit) * unit


class Exchange:
    def __init__(self, first_rows, last_rows, first_cols, last_cols):
        rows = {-1: range(first_rows), 0: range(WLAT), 1: range(WLAT - last_rows, WLAT)}
        cols = {-1: range(first_cols), 0: range(WLON), 1: range(WLON - last_cols, WLON)}
        self.pieces = []
        packed, codes = [], list(range(4 * TOK, 5 * TOK))
        offset = 0
        for dy, dx in ((1, 1), (1, -1), (-1, 1), (-1, -1), (1, 0), (-1, 0), (0, 1), (0, -1)):
            tokens = [(r * WLON + c) * LEV + l for r in rows[dy] for c in cols[dx] for l in range(LEV)]
            if not tokens:
                continue
            size = up_to(len(tokens), 16)
            zone = (1 - dy) * 3 + 1 - dx
            filler = [-1] * (size - len(tokens))
            codes += [zone * TOK + token for token in tokens] + filler
            packed += tokens + filler
            self.pieces.append((dy, dx, offset, size))
            offset += size
        self.sent = offset
        self.held = TOK + offset
        self.codes, self.packed = np.array(codes, np.int32), np.array(packed, np.int32)


def quotient(value, by):
    factor = (1 << 14) // by + 1
    assert all((i * factor) >> 14 == i // by for i in range(TOK + 1))
    return (value * factor) >> 14


def frame_places():
    index = lax.broadcasted_iota(jnp.int32, (TOK, 1), 0)
    place = index >> 1
    row = quotient(place, WLON)
    return row, place - row * WLON, index & 1


def read_codes(down, right):
    row, col, level = frame_places()
    row, col = row + down, col + right
    zone_row = jnp.where(row >= WLAT, 1, 0) - jnp.where(row < 0, 1, 0)
    zone_col = jnp.where(col >= WLON, 1, 0) - jnp.where(col < 0, 1, 0)
    place = (row - zone_row * WLAT) * WLON + col - zone_col * WLON
    return ((zone_row + 1) * 3 + zone_col + 1) * TOK + place * LEV + level


def one_hot(left, right):
    return jnp.where(left == right, 1.0, 0.0).astype(BF16)


def dot(a, b, dims=(((1,), (0,)), ((), ()))):
    return lax.dot_general(a, b, dims, preferred_element_type=F32)


def kernel(
    sizes, starts, halo, mid, out,
    states, final_cot, step_cot, w_qkv, w_out, land_vec, land_sea, ground, shifts, codes,
    result,
    raw, w_qkv_v, w_out_v, land_vec_v, tables_v, shifts_v, codes_v,
    ext_halo, ext_mid, ext_out, send_halo, send_mid, send_out, pick_halo, pick_mid, pick_out, pick_own, pack_mid, pack_out,
    normed_f, proj, att, cot_f, d_proj, d_mixed, direct,
    local_sem, send_sem, recv_sem, go_sem,
):
    n_lat, n_lon = sizes
    features = w_qkv.shape[0]
    quads = HEADS // 4
    wide = features // quads
    step, lat, lon = lax.axis_index("step"), lax.axis_index("lat"), lax.axis_index("lon")
    late = step == 1
    early = step == 0

    def around(dy, dx, other=False):
        return (
            1 - step if other else step,
            lax.rem(lat + (dy + n_lat), n_lat),
            lax.rem(lon + (dx + n_lon), n_lon),
        )

    to_early = [(0, 0)] + [(dy, dx) for dy, dx, _, _ in mid.pieces]
    to_same = sorted(
        {(dy * k, dx * k) for e in halo + out for dy, dx, _, _ in e.pieces for k in (1, -1)}
    )
    sign = 2 * step - 1
    barrier = pltpu.get_barrier_semaphore()
    for dy, dx in to_same:
        pl.semaphore_signal(barrier, inc=1, device_id=around(dy, dx), device_id_type=MESH)
    for dy, dx in to_early:
        pl.semaphore_signal(barrier, inc=1, device_id=around(dy * sign, dx * sign, True), device_id_type=MESH)

    local = [
        pltpu.make_async_copy(src, dst, local_sem.at[i])
        for i, (src, dst) in enumerate((
            (states, raw.at[0]),
            (codes, codes_v),
            (step_cot, raw.at[2]),
            (shifts, shifts_v),
            (land_sea, tables_v.at[0]),
            (ground, tables_v.at[1]),
            (land_vec, land_vec_v),
            (w_qkv, w_qkv_v),
            (w_out, w_out_v),
            (final_cot, raw.at[1]),
        ))
    ]
    (c_state, c_codes, c_step, c_shift, c_land, c_ground, c_vec, c_qkv, c_out, c_final) = local
    for copy in local:
        copy.start()

    def remotes(first, exchange, src, dst, other=False):
        return [
            pltpu.make_async_remote_copy(
                src_ref=src.at[pl.ds(offset, size)], dst_ref=dst.at[pl.ds(TOK + offset, size)],
                send_sem=send_sem.at[first + k], recv_sem=recv_sem.at[first + k],
                device_id=around(dy, dx, other), device_id_type=MESH,
            )
            for k, (dy, dx, offset, size) in enumerate(exchange.pieces)
        ]

    halo_sends = [[remotes(8 * i, halo[half], send_halo.at[i], ext_halo.at[i]) for i in range(2)] for half in range(2)]
    out_sends = [remotes(16, out[half], send_out, ext_out) for half in range(2)]
    mid_sends = [pltpu.make_async_remote_copy(
        src_ref=ext_out.at[pl.ds(0, TOK)], dst_ref=ext_mid.at[pl.ds(0, TOK)],
        send_sem=send_sem.at[32], recv_sem=recv_sem.at[32], device_id=around(0, 0, True), device_id_type=MESH,
    )] + remotes(24, mid, send_mid, ext_mid, True)

    def started(copies):
        for copy in copies:
            copy.start()

    def arrived(copies):
        for copy in copies:
            copy.wait_recv()

    def own_row(first, width):
        return jnp.where(late, codes_v[first + 1 : first + 2, :width], codes_v[first : first + 1, :width])

    def packing(row):
        token = lax.broadcasted_iota(jnp.int32, (TOK, row.shape[1]), 0)
        return one_hot(token, row)

    def clear(target, exchange):
        rows = target.shape[0] - exchange.held
        if rows:
            target[pl.ds(exchange.held, rows)] = jnp.zeros((rows, features), BF16)

    c_codes.wait()
    pack_halo = packing(own_row(8, send_halo.shape[1]))
    c_state.wait()
    ext_halo[0, pl.ds(0, TOK)] = raw[0].reshape(TOK, features)
    send_halo[0] = dot(pack_halo, ext_halo[0, pl.ds(0, TOK)], TN).astype(BF16)
    pl.semaphore_wait(barrier, len(to_same) + len(to_early))

    @pl.when(late)
    def _():
        started(halo_sends[1][0])

    c_step.wait()
    c_final.wait()
    ext_halo[1, pl.ds(0, TOK)] = raw[2 - step].reshape(TOK, features)
    send_halo[1] = dot(pack_halo, ext_halo[1, pl.ds(0, TOK)], TN).astype(BF16)

    @pl.when(late)
    def _():
        direct[...] = raw[2].reshape(TOK, features)
        clear(ext_halo.at[0], halo[1])
        clear(ext_halo.at[1], halo[1])
        clear(ext_out, out[1])

    @pl.when(early)
    def _():
        direct[...] = jnp.zeros((TOK, features), BF16)
        clear(ext_halo.at[0], halo[0])
        clear(ext_halo.at[1], halo[0])
        clear(ext_out, out[0])

    c_shift.wait()
    s_early, s_late = starts
    t_early, t_late = (jnp.where(b >= 6, b - WLON, b) for b in (shifts_v[0, 1], shifts_v[1, 1]))
    s = jnp.where(late, s_late, s_early)
    t = jnp.where(late, t_late, t_early)
    own_codes = lax.broadcasted_iota(jnp.int32, (1, TOK), 1) + 4 * TOK
    read_halo, read_out = read_codes(s, t), read_codes(-s, -t)
    read_mid = read_codes(s_early - s_late, t_early - t_late)
    pick_own[0] = one_hot(read_halo, own_codes)
    pick_own[1] = one_hot(read_mid, own_codes)
    pick_own[2] = one_hot(read_out, own_codes)
    pick_halo[...] = one_hot(read_halo, own_row(0, ext_halo.shape[1] - TOK))
    pick_out[...] = one_hot(read_out, own_row(3, ext_out.shape[0] - TOK))
    pack_out[...] = packing(own_row(11, send_out.shape[0]))
    pack_mid[...] = packing(codes_v[10:11, : mid.sent])
    pick_mid[...] = one_hot(read_mid, codes_v[2:3, : mid.sent])

    row, col, level = frame_places()
    lat_total, lon_total = tables_v.shape[1], tables_v.shape[2]
    at_row = lat * WLAT + s + row
    at_row = jnp.where(at_row < 0, at_row + lat_total, jnp.where(at_row >= lat_total, at_row - lat_total, at_row))
    at_col = lon * WLON + t + col
    at_col = jnp.where(at_col < 0, at_col + lon_total, jnp.where(at_col >= lon_total, at_col - lon_total, at_col))
    c_land.wait()
    c_ground.wait()
    row_pick = one_hot(at_row, lax.broadcasted_iota(jnp.int32, (TOK, lat_total), 1))
    col_pick = at_col == lax.broadcasted_iota(jnp.int32, (TOK, lon_total), 1)

    def looked_up(table):
        lines = dot(row_pick, table.astype(F32).astype(BF16))
        return jnp.sum(jnp.where(col_pick, lines, 0.0), axis=1, keepdims=True)

    both = looked_up(tables_v[0] + 2 * tables_v[1])
    ground_at = jnp.where(both >= 1.5, 1.0, 0.0)
    land = both - 2.0 * ground_at
    key_valid = jnp.where(level.astype(F32) >= ground_at, 1.0, 0.0)
    shift_lat = jnp.where(s < 0, s + WLAT, s)
    window = jnp.where(s < 0, lax.rem(lat + (n_lat - 1), n_lat), lat)
    first_seam = jnp.where(window == n_lat - 1, WLAT - shift_lat, WLAT)
    lane = lax.broadcasted_iota(jnp.int32, (1, 4 * TOK), 1)
    lane = jnp.where(lane >= 2 * TOK, lane - 2 * TOK, lane)
    lane = jnp.where(lane >= TOK, lane - TOK, lane)
    seam_key = jnp.where(row >= first_seam, 1, 0)
    seam_query = jnp.where(quotient(lane >> 1, WLON) >= first_seam, 1, 0)
    allowed = jnp.where(seam_key == seam_query, key_valid, 0.0)
    c_vec.wait()
    c_qkv.wait()

    def picked_own(i, held):
        return dot(pick_own[i], held[pl.ds(0, TOK)])

    def picked(pick, held):
        return dot(pick[...], held[pl.ds(TOK, pick.shape[1])])

    normed_f[...] = picked_own(0, ext_halo.at[0]) + land * land_vec_v[...]
    cot_f[...] = picked_own(0, ext_halo.at[1])

    @pl.when(late)
    def _():
        started(halo_sends[1][1])
        arrived(halo_sends[1][0])
        pl.semaphore_signal(go_sem, inc=1, device_id=around(0, 0, True), device_id_type=MESH)

    @pl.when(early)
    def _():
        pl.semaphore_wait(go_sem, 1)
        started(halo_sends[0][0] + halo_sends[0][1])
        arrived(halo_sends[0][0])

    lifted = normed_f[...] + picked(pick_halo, ext_halo.at[0])
    centred = lifted - jnp.mean(lifted, axis=1, keepdims=True)
    scale = lax.rsqrt(jnp.mean(centred * centred, axis=1, keepdims=True) + 1e-05)
    normed = centred * scale
    normed_f[...] = normed
    projected = dot(normed.astype(BF16), w_qkv_v[...]).astype(BF16)
    for p in range(3 * quads):
        proj[p] = projected[:, p * wide : (p + 1) * wide]
    group = lax.broadcasted_iota(jnp.int32, (TOK, wide), 1) >> 6
    zero = jnp.zeros((TOK, wide), BF16)

    def by_head(quad):
        return jnp.concatenate([jnp.where(group == h, quad, zero) for h in range(4)], axis=0)

    @pl.loop(0, quads)
    def _(p):
        weights = jnp.exp(dot(proj[quads + p], by_head(proj[p] * 0.125), NT)) * allowed
        att[p] = weights * (1.0 / jnp.sum(weights, axis=0, keepdims=True))

    @pl.when(late)
    def _():
        arrived(halo_sends[1][1])

    @pl.when(early)
    def _():
        arrived(halo_sends[0][1])

    cot_f[...] += picked(pick_halo, ext_halo.at[1])
    c_out.wait()

    @pl.when(early)
    def _():
        arrived(mid_sends[:1])
        cot_f[...] += picked_own(1, ext_mid)
        arrived(mid_sends[1:])
        cot_f[...] += picked(pick_mid, ext_mid)

    cot_w = cot_f[...].astype(BF16)

    d_all = dot(cot_w, w_out_v[...], NT).astype(BF16)
    for p in range(quads):
        d_mixed[p] = d_all[:, p * wide : (p + 1) * wide]

    @pl.loop(0, quads)
    def _(p):
        d_heads = by_head(d_mixed[p])
        attention = att[p]
        inner = attention * dot(proj[2 * quads + p], d_heads, NT)
        d_scores = (inner - attention * jnp.sum(inner, axis=0, keepdims=True)).astype(BF16)
        d_each = dot(d_scores, proj[quads + p], TN)
        d_query = d_each[:TOK]
        for h in range(1, 4):
            d_query = jnp.where(group == h, d_each[h * TOK : (h + 1) * TOK], d_query)
        d_proj[p] = (d_query * 0.125).astype(BF16)
        d_proj[quads + p] = dot(d_scores, by_head(proj[p] * 0.125)).astype(BF16)
        d_proj[2 * quads + p] = dot(attention.astype(BF16), d_heads).astype(BF16)

    d_all = jnp.concatenate([d_proj[p] for p in range(3 * quads)], axis=1)
    d_normed = dot(d_all, w_qkv_v[...], NT).astype(BF16).astype(F32)
    normed = normed_f[...]
    along = jnp.mean(d_normed * normed, axis=1, keepdims=True)
    total = cot_w.astype(F32) + scale * (d_normed - jnp.mean(d_normed, axis=1, keepdims=True) - normed * along)
    ext_out[pl.ds(0, TOK)] = total.astype(BF16)

    @pl.when(late)
    def _():
        mid_sends[0].start()
        send_mid[...] = dot(pack_mid[...], ext_out[pl.ds(0, TOK)], TN).astype(BF16)
        started(mid_sends[1:])
        for copy in mid_sends:
            copy.wait_send()

    send_out[...] = dot(pack_out[...], ext_out[pl.ds(0, TOK)], TN).astype(BF16)

    @pl.when(late)
    def _():
        started(out_sends[1])

    @pl.when(early)
    def _():
        started(out_sends[0])

    normed_f[...] = picked_own(2, ext_out) + direct[...].astype(F32)

    @pl.when(late)
    def _():
        arrived(out_sends[1])

    @pl.when(early)
    def _():
        arrived(out_sends[0])

    home = normed_f[...] + picked(pick_out, ext_out)
    result[...] = home.astype(BF16).reshape(result.shape)

    @pl.when(late)
    def _():
        for copy in halo_sends[1][0] + halo_sends[1][1] + out_sends[1]:
            copy.wait_send()

    @pl.when(early)
    def _():
        for copy in halo_sends[0][0] + halo_sends[0][1] + out_sends[0]:
            copy.wait_send()


def variant(sizes, number, starts, states, final_cot, step_cot, w_qkv, w_out, land_vec, land_sea, ground, shifts):
    before, after = [max(-start, 0) for start in starts], [max(start, 0) for start in starts]
    apart = starts[0] - starts[1]
    halo = [Exchange(after[half], before[half], 5, 6) for half in range(2)]
    mid = Exchange(max(apart, 0), max(-apart, 0), 6, 6)
    out = [Exchange(before[half], after[half], 6, 5) for half in range(2)]
    features = w_qkv.shape[0]
    codes = np.full((16, 512), -1, np.int32)
    for i, e in enumerate(halo + [mid] + out):
        codes[i, : e.sent] = e.codes[TOK:]
        codes[8 + i, : e.sent] = e.packed
    halo_held, halo_sent = max(e.held for e in halo), max(e.sent for e in halo)
    out_held, out_sent = max(e.held for e in out), max(e.sent for e in out)
    held_spec = pl.BlockSpec(memory_space=pltpu.HBM)

    def field(*shape):
        return pltpu.VMEM(shape, BF16)

    def home(block):
        return jnp.moveaxis(block, 0, 2).reshape(TOK // LEV, LEV, features)

    gradient = pl.pallas_call(
        functools.partial(kernel, sizes, starts, halo, mid, out),
        out_shape=jax.ShapeDtypeStruct((TOK // LEV, LEV, features), BF16),
        in_specs=[held_spec] * 10,
        out_specs=pl.BlockSpec(memory_space=pltpu.VMEM),
        scratch_shapes=[
            field(3, TOK // LEV, LEV, features),
            field(*w_qkv.shape),
            field(*w_out.shape),
            pltpu.VMEM((1, features), F32),
            pltpu.VMEM((2,) + land_sea.shape, jnp.int32),
            pltpu.SMEM(shifts.shape, jnp.int32),
            pltpu.VMEM(codes.shape, jnp.int32),
            field(2, halo_held, features),
            field(mid.held, features),
            field(out_held, features),
            field(2, halo_sent, features),
            field(mid.sent, features),
            field(out_sent, features),
            field(TOK, halo_sent),
            field(TOK, mid.sent),
            field(TOK, out_sent),
            field(3, TOK, TOK),
            field(TOK, mid.sent),
            field(TOK, out_sent),
            pltpu.VMEM((TOK, features), F32),
            field(3 * HEADS // 4, TOK, 4 * features // HEADS),
            pltpu.VMEM((HEADS // 4, TOK, 4 * TOK), F32),
            pltpu.VMEM((TOK, features), F32),
            field(3 * HEADS // 4, TOK, 4 * features // HEADS),
            field(HEADS // 4, TOK, 4 * features // HEADS),
            field(TOK, features),
            pltpu.SemaphoreType.DMA((10,)),
            pltpu.SemaphoreType.DMA((33,)),
            pltpu.SemaphoreType.DMA((33,)),
            pltpu.SemaphoreType.REGULAR,
        ],
        compiler_params=pltpu.CompilerParams(
            collective_id=number, has_side_effects=True, vmem_limit_bytes=60 * 1024 * 1024
        ),
    )(
        home(states[0]), home(final_cot), home(step_cot), w_qkv, w_out, land_vec.reshape(1, features),
        land_sea, ground, shifts, jnp.asarray(codes),
    )
    return jnp.moveaxis(gradient.reshape(WLAT, WLON, LEV, features), 2, 0)[None]


def per_device(sizes, *operands):
    others = (1, 2, 3 - WLAT, 4 - WLAT, -1)
    pairs = [(start, -1) for start in others] + [(-1, start) for start in others[:-1]]
    shifts = operands[-1]
    one, five = np.array([[1, 0], [1, 0]], np.int32), np.array([[0, 0], [5, 0]], np.int32)
    case = jnp.sum((shifts - 3) * one + jnp.minimum(5 - shifts, 1) * five)
    cases = [functools.partial(variant, sizes, number, pair) for number, pair in enumerate(pairs)]
    return lax.switch(case, cases, *operands)


def solution(mesh):
    return jax.shard_map(
        functools.partial(per_device, (mesh.shape["lat"], mesh.shape["lon"])),
        mesh=mesh,
        in_specs=(
            P("step", None, "lat", "lon", None),
            P(None, "lat", "lon", None),
            P(None, "lat", "lon", None),
            P(),
            P(),
            P(),
            P(),
            P(),
            P(),
        ),
        out_specs=P("step", None, "lat", "lon", None),
        check_vma=False,
    )
```
